256 devices in a mesh: section: 4 (over y), row: 16 (over z, core), col: 4 (over x).
Axes of the slice: x: 4, y: 4, z: 8, core: 2. Of those that a mesh axis runs over, the one named last changes fastest.
Arguments:
- inputs: bfloat16 [1024, 12288], P('section', ('col', 'row')), may hold values from -6 to 6
- out_grad: bfloat16 [1024, 12288], P('section', ('col', 'row')), may hold values from -1.5 to 1.5
- w_up: bfloat16 [12288, 24576], P('col', ('section', 'row')), may hold values from -0.0546875 to 0.0546875
- w_down: bfloat16 [12288, 24576], P('col', ('section', 'row')), may hold values from -0.0546875 to 0.0546875
Outputs:
- input_grad: float32 [1024, 12288], P('section', ('col', 'row'))
- w_up_grad: bfloat16 [12288, 24576], P('col', ('section', 'row'))
- w_down_grad: bfloat16 [12288, 24576], P('col', ('section', 'row'))
The draws below stay inside these ranges and needn't reach their ends.
All inputs are finite; a program needn't handle non-finite values.
Results may differ from the reference program's by a relative error of at most 0.02.
Values may be sent and summed in bfloat16 or wider, within the bound.
A program may use at most 192 MiB of HBM per device.

```python
import jax
import jax.numpy as jnp

D = 12288
FF = 24576
TOKENS = 1024


def level_of(own_key, extent, cuts, least, high):
    loudness, own = 1.0, jax.random.fold_in(own_key, 6)
    for dim, parts in cuts:
        draws = jnp.exp(jax.random.uniform(jax.random.fold_in(own, dim), (parts,), jnp.float32, least / len(cuts), high / len(cuts)))
        loudness = loudness * jnp.repeat(draws, extent[dim] // parts).reshape([-1 if axis == dim else 1 for axis in range(len(extent))])
    return loudness


def bell_draw(rng, extent, deviation, reach, split=(), held_as=jnp.bfloat16):
    result = jax.random.normal(rng, extent, jnp.float32) * deviation
    if len(split) > 0:
        result = level_of(rng, extent, split, -0.22, 0.18) * result
    return jnp.clip(result, min=-reach, max=reach).astype(held_as)


def setup_inputs(seed: int = 0) -> dict:
    key_list = jax.random.split(jax.random.key(seed), 5)
    return {
        "inputs": bell_draw(key_list[0], (TOKENS, D), 1.0, 6.0, ((0, 4), (1, 64))),
        "out_grad": bell_draw(key_list[1], (TOKENS, D), 0.25, 1.5, ((0, 4), (1, 64))),
        "w_up": bell_draw(key_list[2], (D, FF), D ** -0.5, 0.0546875, ((0, 4), (1, 64))),
        "w_down": bell_draw(key_list[3], (D, FF), D ** -0.5, 0.0546875, ((0, 4), (1, 64))),
    }


coeff = 0.7978845608028654


def gelu_pair(pre, back):
    inner = coeff * (pre + 0.044715 * pre * pre * pre)
    tanh_val = jnp.tanh(inner)
    act = 0.5 * pre * (1.0 + tanh_val)
    slope = 0.5 * (1.0 + tanh_val) + 0.5 * pre * (1.0 - tanh_val * tanh_val) * coeff * (1.0 + 3.0 * 0.044715 * pre * pre)
    return act.astype(jnp.bfloat16), (back * slope).astype(jnp.bfloat16)


def reference(inputs, out_grad, w_up, w_down):
    pre = jnp.dot(inputs, w_up, preferred_element_type=jnp.float32)
    back = jnp.dot(out_grad, w_down, preferred_element_type=jnp.float32)
    act, grad_pre = gelu_pair(pre, back)
    w_down_grad = jnp.dot(out_grad.T, act, preferred_element_type=jnp.float32).astype(jnp.bfloat16)
    w_up_grad = jnp.dot(inputs.T, grad_pre, preferred_element_type=jnp.float32).astype(jnp.bfloat16)
    input_grad = jnp.dot(grad_pre, w_up.T, preferred_element_type=jnp.float32)
    return input_grad, w_up_grad, w_down_grad
```

```python
import functools

import jax
import jax.numpy as jnp
from jax import lax
from jax.experimental import pallas as pl
from jax.experimental.pallas import tpu as pltpu
from jax.sharding import PartitionSpec as P

coeff = 0.7978845608028654
f32 = jnp.float32
bf16 = jnp.bfloat16
R, L = 0, 1
N_SEMS = 224

Z_REL = (0, 1, -1, 2, -2, 3, -3, 4)
GATHER_SRC = {R: (0, 2, 4, 6), L: (0, 1, 3, 5)}
GATHER_DST = {R: (2, 4, 6, 7), L: (1, 3, 5, 7)}
GROUPS = {1: (0, 3), 2: (3, 5), 3: (5, 7), 4: (7, 8)}
SUM_SRC = {R: (7, 5, 3, 1), L: (7, 6, 4, 2)}
SUM_DST = {R: (5, 3, 1, 0), L: (6, 4, 2, 0)}


def gelu_pair(pre, back):
    inner = coeff * (pre + 0.044715 * pre * pre * pre)
    tanh_val = jnp.tanh(inner)
    act = 0.5 * pre * (1.0 + tanh_val)
    slope = 0.5 * (1.0 + tanh_val) + 0.5 * pre * (1.0 - tanh_val * tanh_val) * coeff * (
        1.0 + 3.0 * 0.044715 * pre * pre
    )
    return act, back * slope


def kernel(
    x_in, d_in, wu_in, wd_in,
    ig_out, gu_out, gd_out,
    X, D, WU, UT, DT, WG, PB, RL, FN, AGB, AT, IGP, CR, ZR, YR, YF,
    send_sems, recv_sems, local_sems,
):
    n_sec, n_row, n_col = (lax.axis_size(a) for a in ("section", "row", "col"))
    n_z = n_row // 2
    s, r, c = (lax.axis_index(a) for a in ("section", "row", "col"))
    z, core = r // 2, r % 2

    def turn(i, by, n):
        return lax.rem(i + (by + n), n)

    zdev = {d: {"row": turn(z, by, n_z) * 2 + core} for d, by in ((R, 1), (L, -1))}
    ydev = {d: {"section": turn(s, by, n_sec)} for d, by in ((R, 1), (L, -1))}
    xdev = {d: {"col": turn(c, by, n_col)} for d, by in ((R, 1), (L, -1))}
    partner = {"row": z * 2 + (1 - core)}

    barrier = pltpu.get_barrier_semaphore()
    for dev in (*zdev.values(), *ydev.values(), *xdev.values(), partner):
        pl.semaphore_signal(
            barrier, inc=1, device_id=dev, device_id_type=pl.DeviceIdType.MESH
        )

    own_x = pltpu.make_async_copy(x_in, X.at[0, 0, 0], local_sems.at[0])
    own_d = pltpu.make_async_copy(d_in, D.at[0, 0, 0], local_sems.at[1])
    own_x.start()
    own_d.start()
    WD = WG.at[1]

    def block_rows(slot, other):
        row = turn(z, Z_REL[slot], n_z) * 2 + (1 - core if other else core)
        return pl.ds(pl.multiple_of(row * 192, 192), 192)

    for src, dst, sem in ((wu_in, WU, 2), (wd_in, WD, 3)):
        for slot in range(8):
            for other in range(2):
                pltpu.make_async_copy(
                    src.at[block_rows(slot, other)], dst.at[slot, other], local_sems.at[sem]
                ).start()

    pl.semaphore_wait(barrier, 7)

    started = {}
    arrived = set()

    def start(name, src, dst, dev):
        i = len(started)
        assert i < N_SEMS and name not in started
        started[name] = pltpu.make_async_remote_copy(
            src_ref=src,
            dst_ref=dst,
            send_sem=send_sems.at[i],
            recv_sem=recv_sems.at[i],
            device_id=dev,
            device_id_type=pl.DeviceIdType.MESH,
        )
        started[name].start()

    def need(*names):
        for name in names:
            if name not in arrived:
                arrived.add(name)
                started[name].wait_recv()

    bufs = {"X": X, "D": D}
    far_dir = {("X", 0): R, ("D", 0): L, ("D", 1): R, ("D", 2): L, ("D", 3): R}

    def zsend(nm, k, h, src=None):
        for d in (R, L):
            if h < 4 or far_dir[nm, k] == d:
                b = bufs[nm]
                a = b.at[k, GATHER_SRC[d][h - 1], 0] if src is None else src
                start(f"{nm}{k}z{h}{d}", a, b.at[k, GATHER_DST[d][h - 1], 0], zdev[d])

    def zgot(nm, k, h):
        for d in (R, L):
            if h < 4 or far_dir[nm, k] == d:
                need(f"{nm}{k}z{h}{d}")
        if h < 4:
            zsend(nm, k, h + 1)
        lo, hi = GROUPS[h]
        b = bufs[nm]
        if nm == "X":
            start(f"Xy{h}{R}", X.at[0, lo:hi, 0], X.at[2, lo:hi, 0], ydev[R])
            start(f"Xy{h}{L}", X.at[0, lo:hi, 0], X.at[1, lo:hi, 0], ydev[L])
        start(f"{nm}{k}c{h}", b.at[k, lo:hi, 0], b.at[k, lo:hi, 1], partner)

    def ygot(h):
        need(f"Xy{h}{R}", f"Xy{h}{L}")
        lo, hi = GROUPS[h]
        if h == 1:
            start("Xf0", X.at[2, 0:3, 0], X.at[3, 0:3, 0], ydev[R])
        if h == 3:
            start("Xf1", X.at[1, 3:7, 0], X.at[3, 3:7, 0], ydev[L])
        if h == 4:
            start("Xf2", X.at[2, 7:8, 0], X.at[3, 7:8, 0], ydev[R])
        start(f"Xyc{h}", X.at[1:3, lo:hi, 0], X.at[1:3, lo:hi, 1], partner)

    def fgot(i):
        need(f"Xf{i}")
        lo, hi = ((0, 3), (3, 7), (7, 8))[i]
        start(f"Xfc{i}", X.at[3, lo:hi, 0], X.at[3, lo:hi, 1], partner)

    def transpose(src, dst):
        @pl.loop(0, 4)
        def _(p):
            dst[p] = src[pl.ds(p * 2, 2)].reshape(768, 384).T

    def hidden(owner):
        return pl.ds(pl.multiple_of(owner * 96, 96), 96)

    c_next, c_prev, c_far = turn(c, 1, n_col), turn(c, -1, n_col), turn(c, 2, n_col)

    def partial(k):
        if k == 0:
            need(*(f"{nm}0c{h}" for nm in "XD" for h in (1, 2, 3, 4)))
        elif k < 3:
            need(*(f"Xyc{h}" for h in (1, 2, 3, 4)))
            need(*(f"D{k}c{h}" for h in (1, 2, 3, 4)))
        else:
            need(*(f"Xfc{i}" for i in range(3)))
            need(*(f"D{k}c{h}" for h in (1, 2, 3, 4)))
        for j, (b, w) in enumerate(((X, UT), (D, DT))):
            acc = jnp.zeros((384, 256), f32)
            for p in range(4):
                acc += jnp.dot(
                    w[p], b[k, 2 * p : 2 * p + 2].reshape(768, 256), preferred_element_type=f32
                )
            PB[k, j] = acc.astype(bf16)
        start(f"r{k}{R}", PB.at[k, 0, hidden(c_far)], RL.at[k, 0], xdev[R])
        start(f"r{k}{L}", PB.at[k, 1, hidden(c_far)], RL.at[k, 1], xdev[L])
        start(f"f{k}b{R}", PB.at[k, 1, hidden(c_next)], FN.at[k, 0, 1], xdev[R])
        start(f"f{k}p{L}", PB.at[k, 0, hidden(c_prev)], FN.at[k, 1, 0], xdev[L])

    def relay(k):
        for j, d, rows, tag in ((0, R, hidden(c_next), "p"), (1, L, hidden(c_prev), "b")):
            need(f"r{k}{d}")
            PB[k, j, rows] = (PB[k, j, rows].astype(f32) + RL[k, j].astype(f32)).astype(bf16)
            start(f"f{k}{tag}{d}", PB.at[k, j, rows], FN.at[k, d, j], xdev[d])

    def gelu(k):
        need(*(f"f{k}{tag}{d}" for tag in "pb" for d in (R, L)))
        rows = hidden(c)
        pre, back = (
            PB[k, j, rows].astype(f32) + FN[k, 0, j].astype(f32) + FN[k, 1, j].astype(f32)
            for j in range(2)
        )
        act, grad = gelu_pair(pre, back)
        AGB[k, 0, rows] = act.astype(bf16)
        AGB[k, 1, rows] = grad.astype(bf16)
        for d in (R, L):
            start(f"a{k}{d}", AGB.at[k, :, rows], AGB.at[k, :, rows], xdev[d])

    def spread(k):
        need(f"a{k}{R}")
        rows = hidden(c_prev)
        start(f"h{k}{R}", AGB.at[k, 0, rows], AGB.at[k, 0, rows], xdev[R])
        need(f"a{k}{L}")
        rows = hidden(c_next)
        start(f"h{k}{L}", AGB.at[k, 1, rows], AGB.at[k, 1, rows], xdev[L])

    def ig_part(k):
        need(f"h{k}{R}", f"h{k}{L}")

        @pl.loop(0, 4)
        def _(p):
            w = WU[pl.ds(p * 2, 2)].reshape(768, 384)
            g = jnp.dot(w, AGB[k, 1], preferred_element_type=f32)
            IGP[k, pl.ds(p * 2, 2)] = g.astype(bf16).reshape(2, 2, 192, 256)

        start(f"C{k}", IGP.at[k, :, 1], CR.at[k], partner)

    def sum_hops(k, d):
        return (0, 1, 2, 3) if (k % 2 == 0) == (d == R) else (1, 2, 3)

    def zsum_send(k, d, j):
        start(f"S{k}{d}{j}", IGP.at[k, SUM_SRC[d][j], 0], ZR.at[k, d, j], zdev[d])

    def core_sum(k):
        need(f"C{k}")
        for slot in (7, 6, 5, 4, 3, 2, 1, 0):
            IGP[k, slot, 0] = (IGP[k, slot, 0].astype(f32) + CR[k, slot].astype(f32)).astype(bf16)
            for d in (R, L):
                j = sum_hops(k, d)[0]
                if SUM_SRC[d][j] == slot:
                    zsum_send(k, d, j)

    def zsum(k, j):
        for d in (R, L):
            if j in sum_hops(k, d):
                need(f"S{k}{d}{j}")
                slot = SUM_DST[d][j]
                if j < 3:
                    IGP[k, slot, 0] = (
                        IGP[k, slot, 0].astype(f32) + ZR[k, d, j].astype(f32)
                    ).astype(bf16)
                    zsum_send(k, d, j + 1)

    lower, upper = slice(0, 96), slice(96, 192)

    def zsum_end(k):
        zsum(k, 3)
        total = IGP[k, 0, 0].astype(f32) + ZR[k, 0, 3].astype(f32) + ZR[k, 1, 3].astype(f32)
        if k == 0:
            ig_out[...] = total
            return
        IGP[k, 0, 0] = total.astype(bf16)
        if k == 1:
            start("yfb", IGP.at[1, 0, 0, upper], YF.at[0, upper], ydev[R])
        elif k == 2:
            start("yfc", IGP.at[2, 0, 0, lower], YF.at[1, lower], ydev[L])
        else:
            start("yr0", IGP.at[3, 0, 0, lower], YR.at[0], ydev[R])
            start("yr1", IGP.at[3, 0, 0, upper], YR.at[1], ydev[L])

    def ysum():
        for d, k, part in ((R, 1, lower), (L, 2, upper)):
            need(f"yr{d}")
            IGP[k, 0, 0, part] = (
                IGP[k, 0, 0, part].astype(f32) + YR[d].astype(f32)
            ).astype(bf16)
            start(f"yf{d}", IGP.at[k, 0, 0, part], YF.at[d, part], ydev[d])

    def ysum_end():
        need("yfb", "yfc", "yf0", "yf1")
        ig_out[...] = ig_out[...] + YF[0].astype(f32) + YF[1].astype(f32)

    def turn_acts():
        for k in range(4):
            for j in range(2):
                AT[j, k] = AGB[k, j].T

    def weight_grad(which, slots):
        b, j, out = ((X, 1, gu_out), (D, 0, gd_out))[which]
        for slot in slots:
            acc = jnp.zeros((384, 384), f32)
            for k in range(4):
                acc += jnp.dot(
                    b[k, slot].reshape(384, 256), AT[j, k], preferred_element_type=f32
                )
            WG[which, slot] = acc.astype(bf16).reshape(2, 192, 384)
            for other in range(2):
                pltpu.make_async_copy(
                    WG.at[which, slot, other],
                    out.at[block_rows(slot, other)],
                    local_sems.at[4 + which],
                ).start()

    zsend("X", 0, 1, x_in)
    zsend("D", 0, 1, d_in)
    start("Dy0", d_in, D.at[2, 0, 0], ydev[R])
    start("Dy1", d_in, D.at[1, 0, 0], ydev[L])
    own_x.wait()
    own_d.wait()
    pltpu.make_async_copy(WU, WU, local_sems.at[2]).wait()
    transpose(WU, UT)
    zgot("X", 0, 1)
    zgot("D", 0, 1)
    need("Dy0", "Dy1")
    start("Dy2", D.at[2, 0, 0], D.at[3, 0, 0], ydev[R])
    pltpu.make_async_copy(WD, WD, local_sems.at[3]).wait()
    transpose(WD, DT)
    zgot("X", 0, 2)
    zgot("D", 0, 2)
    zsend("D", 1, 1)
    ygot(1)
    need("Dy2")
    zgot("X", 0, 3)
    zgot("D", 0, 3)
    zgot("D", 1, 1)
    zsend("D", 2, 1)
    ygot(2)
    zgot("X", 0, 4)
    zgot("D", 0, 4)
    zgot("D", 1, 2)
    zgot("D", 2, 1)
    ygot(3)
    fgot(0)
    partial(0)
    zgot("D", 1, 3)
    zgot("D", 2, 2)
    zsend("D", 3, 1)
    ygot(4)
    relay(0)
    zgot("D", 1, 4)
    zgot("D", 2, 3)
    zgot("D", 3, 1)
    gelu(0)
    fgot(1)
    partial(1)
    zgot("D", 2, 4)
    zgot("D", 3, 2)
    spread(0)
    relay(1)
    partial(2)
    fgot(2)
    zgot("D", 3, 3)
    ig_part(0)
    gelu(1)
    relay(2)
    zgot("D", 3, 4)
    core_sum(0)
    spread(1)
    partial(3)
    gelu(2)
    zsum(0, 0)
    ig_part(1)
    relay(3)
    zsum(0, 1)
    core_sum(1)
    spread(2)
    zsum(0, 2)
    gelu(3)
    ig_part(2)
    zsum(1, 0)
    zsum_end(0)
    core_sum(2)
    spread(3)
    zsum(1, 1)
    zsum(2, 0)
    ig_part(3)
    zsum(1, 2)
    zsum(2, 1)
    core_sum(3)
    turn_acts()
    zsum_end(1)
    zsum(2, 2)
    weight_grad(0, (0, 1))
    zsum(3, 0)
    zsum_end(2)
    weight_grad(0, (2, 3, 4))
    zsum(3, 1)
    weight_grad(0, (5, 6, 7))
    zsum(3, 2)
    weight_grad(1, (0, 1, 2))
    zsum_end(3)
    weight_grad(1, (3, 4, 5))
    ysum()
    weight_grad(1, (6, 7))
    ysum_end()
    assert arrived == set(started)
    for copy in started.values():
        copy.wait_send()
    for which in range(2):
        pltpu.make_async_copy(WG.at[which], WG.at[which], local_sems.at[4 + which]).wait()


def on_device(inputs, out_grad, w_up, w_down):
    any_spec = pl.BlockSpec(memory_space=pl.ANY)
    ig_t, gu, gd = pl.pallas_call(
        kernel,
        out_shape=(
            jax.ShapeDtypeStruct((192, 256), f32),
            jax.ShapeDtypeStruct((3072, 384), bf16),
            jax.ShapeDtypeStruct((3072, 384), bf16),
        ),
        in_specs=[any_spec] * 4,
        out_specs=(pl.BlockSpec(memory_space=pltpu.VMEM), any_spec, any_spec),
        scratch_shapes=[
            pltpu.VMEM((4, 8, 2, 192, 256), bf16),
            pltpu.VMEM((4, 8, 2, 192, 256), bf16),
            pltpu.VMEM((8, 2, 192, 384), bf16),
            pltpu.VMEM((4, 384, 768), bf16),
            pltpu.VMEM((4, 384, 768), bf16),
            pltpu.VMEM((2, 8, 2, 192, 384), bf16),
            pltpu.VMEM((4, 2, 384, 256), bf16),
            pltpu.VMEM((4, 2, 96, 256), bf16),
            pltpu.VMEM((4, 2, 2, 96, 256), bf16),
            pltpu.VMEM((4, 2, 384, 256), bf16),
            pltpu.VMEM((2, 4, 256, 384), bf16),
            pltpu.VMEM((4, 8, 2, 192, 256), bf16),
            pltpu.VMEM((4, 8, 192, 256), bf16),
            pltpu.VMEM((4, 2, 4, 192, 256), bf16),
            pltpu.VMEM((2, 96, 256), bf16),
            pltpu.VMEM((2, 192, 256), bf16),
            pltpu.SemaphoreType.DMA((N_SEMS,)),
            pltpu.SemaphoreType.DMA((N_SEMS,)),
            pltpu.SemaphoreType.DMA((6,)),
        ],
        compiler_params=pltpu.CompilerParams(
            collective_id=0, has_side_effects=True, vmem_limit_bytes=58 * 2**20
        ),
        cost_estimate=pl.CostEstimate(
            flops=5 * 2 * 1024 * 3072 * 384, bytes_accessed=10_000_000, transcendentals=98304
        ),
        name="ffn_backward",
    )(inputs.T, out_grad.T, w_up, w_down)
    return ig_t.T, gu, gd


def solution(mesh):
    return jax.shard_map(
        on_device,
        mesh=mesh,
        in_specs=(
            P("section", ("col", "row")),
            P("section", ("col", "row")),
            P("col", ("section", "row")),
            P("col", ("section", "row")),
        ),
        out_specs=(
            P("section", ("col", "row")),
            P("col", ("section", "row")),
            P("col", ("section", "row")),
        ),
        check_vma=False,
    )
```

```python
import functools

import jax
import jax.numpy as jnp
from jax import lax
from jax.experimental import pallas as pl
from jax.experimental.pallas import tpu as pltpu
from jax.sharding import PartitionSpec as P

coeff = 0.7978845608028654
f32 = jnp.float32
bf16 = jnp.bfloat16
R, L = 0, 1
SEND_SEMS = 64
RECV_SEMS = 153

Z_REL = (0, 1, -1, 2, -2, 3, -3, 4)
GATHER_SRC = {R: (0, 2, 4, 6), L: (0, 1, 3, 5)}
GATHER_DST = {R: (2, 4, 6, 7), L: (1, 3, 5, 7)}
GROUPS = {1: (0, 3), 2: (3, 5), 3: (5, 7), 4: (7, 8)}
SUM_SRC = {R: (7, 5, 3, 1), L: (7, 6, 4, 2)}
SUM_DST = {R: (5, 3, 1, 0), L: (6, 4, 2, 0)}
X_FAR = ((0, 3), (3, 7), (7, 8))
D_FAR = ((5, 6), (6, 8))
Y_FIRST = ((1, 0), (2, 0), (1, 1), (2, 1))
CHUNKS = ((0, 0, 256), (1, 0, 256), (2, 0, 256), (3, 0, 256))
WIDE = 4
BUFS = ("PB", "RL", "FN", "AGB", "IGP", "CR", "ZR", "YF")


def gelu_pair(pre, back):
    inner = coeff * (pre + 0.044715 * pre * pre * pre)
    tanh_val = jnp.tanh(inner)
    act = 0.5 * pre * (1.0 + tanh_val)
    slope = 0.5 * (1.0 + tanh_val) + 0.5 * pre * (1.0 - tanh_val * tanh_val) * coeff * (
        1.0 + 3.0 * 0.044715 * pre * pre
    )
    return act, back * slope


class Plan:
    def __init__(self, k):
        self.k = k
        self.tasks = {}
        self.groups = {}
        self.regions = {}
        self.gather()
        self.middle()
        self.input_grad()
        self.weight_grads()

    def group(self, name, copies, region):
        self.groups.update({copy: name for copy in copies})
        self.regions[name] = region

    def task(self, name, needs=(), after=(), do=None, sends=()):
        assert name not in self.tasks
        self.tasks[name] = (tuple(needs), tuple(after), do, tuple(sends))

    def gather(self):
        k = self.k
        last = {("X", 0): (4, 3), ("D", 0): (3, 4), ("D", 1): (4, 3), ("D", 2): (3, 4), ("D", 3): (2, 2)}

        def hop(nm, sec, h, d):
            link = ("z", d)

            def refs():
                b = getattr(k, nm)
                src = b.at[sec, GATHER_SRC[d][h - 1], 0]
                if sec == 0 and h == 1:
                    src = k.x_in if nm == "X" else k.d_in
                return src, b.at[sec, GATHER_DST[d][h - 1], 0]

            return (f"{nm}{sec}z{h}{d}", link, 1, refs)

        def move(name, link, nm, sec, to, lo, hi, half=(0, 0)):
            def refs():
                b = getattr(k, nm)
                return b.at[sec, lo:hi, half[0]], b.at[to, lo:hi, half[1]]

            n = (hi - lo) * (2 if isinstance(sec, slice) else 1)
            return (name, link, n, refs)

        def hand(nm, sec, tag, lo, hi):
            return move(f"{nm}{sec}c{tag}", ("p", 0), nm, sec, sec, lo, hi, (0, 1))

        self.task(
            "go",
            sends=[hop(nm, 0, 1, d) for nm in "XD" for d in (R, L)]
            + [
                ("DyR", ("y", R), 1, lambda: (k.d_in, k.D.at[2, 0, 0])),
                ("DyL", ("y", L), 1, lambda: (k.d_in, k.D.at[1, 0, 0])),
            ],
        )
        self.task("own", after=["go"], do=lambda: k.own_wait())
        for j in range(2):
            self.task(f"t{j}", after=["own"], do=lambda j=j: k.transpose(j))
        self.task("D1s", ["DyL"], ["own"], sends=[hop("D", 1, 1, d) for d in (R, L)])
        self.task(
            "D2s",
            ["DyR"],
            ["own"],
            sends=[
                ("Dy2", ("y", R), 1, lambda: (k.D.at[2, 0, 0], k.D.at[3, 0, 0])),
                *(hop("D", 2, 1, d) for d in (R, L)),
            ],
        )
        self.task("D3s", ["Dy2"], ["own"], sends=[hop("D", 3, 1, d) for d in (R, L)])
        for (nm, sec), hops in last.items():
            for d in (R, L):
                for h in range(1, hops[d] + 1):
                    more = [hop(nm, sec, h + 1, d)] if h < hops[d] else []
                    self.task(f"{nm}{sec}z{h}{d}", [f"{nm}{sec}z{h}{d}"], ["own"], sends=more)
            for h, (lo, hi) in GROUPS.items():
                got = [f"{nm}{sec}z{h}{d}" for d in (R, L) if h <= hops[d]]
                if not got:
                    continue
                sends = []
                if nm == "X":
                    sends.append(move(f"Xy{h}{R}", ("y", R), "X", 0, 2, lo, hi))
                    sends.append(move(f"Xy{h}{L}", ("y", L), "X", 0, 1, lo, hi))
                sends.append(hand(nm, sec, h, lo, hi))
                if nm == "D" and sec == 2 and h == 3:
                    sends.insert(0, move("Df0", ("y", R), "D", 2, 3, *D_FAR[0]))
                if nm == "D" and sec == 1 and h == 4:
                    got.append("D1g3")
                    sends.insert(0, move("Df1", ("y", L), "D", 1, 3, *D_FAR[1]))
                if nm == "D" and sec > 0:
                    got.append(f"D{sec}s")
                self.task(f"{nm}{sec}g{h}", after=got, sends=sends)
        for h, (lo, hi) in GROUPS.items():
            sends = []
            if h == 1:
                sends.append(move("Xf0", ("y", R), "X", 2, 3, *X_FAR[0]))
            if h == 3:
                sends.append(move("Xf1", ("y", L), "X", 1, 3, *X_FAR[1]))
            if h == 4:
                sends.append(move("Xf2", ("y", R), "X", 2, 3, *X_FAR[2]))
            sends.append(move(f"Xyc{h}", ("p", 0), "X", slice(1, 3), slice(1, 3), lo, hi, (0, 1)))
            prior = ["own"] if h == 1 else [f"Xy{h - 1}"]
            self.task(f"Xy{h}", [f"Xy{h}{R}", f"Xy{h}{L}"], prior, sends=sends)
        for nm, far in (("X", X_FAR), ("D", D_FAR)):
            for i, (lo, hi) in enumerate(far):
                self.task(
                    f"{nm}f{i}", [f"{nm}f{i}"], ["own"], sends=[hand(nm, 3, f"f{i}", lo, hi)]
                )
        self.has = {
            (nm, sec): [
                *(f"{nm}{sec}g{h}" for h in GROUPS if f"{nm}{sec}g{h}" in self.tasks),
                *((f"{nm}f{i}" for i in range(len(far))) if sec == 3 else ()),
                *((f"Xy{h}" for h in GROUPS) if nm == "X" and sec in (1, 2) else ()),
            ]
            for nm, far in (("X", X_FAR), ("D", D_FAR))
            for sec in range(4)
        }
        self.hands = {}
        for (nm, sec), names in self.has.items():
            copies = []
            for n in names:
                copies += [c[0] for c in self.tasks[n][3] if c[1][0] == "p"]
            self.hands[nm, sec] = copies
            at = slice(1, 3) if nm == "X" and sec in (1, 2) else sec
            self.group(f"{nm}{at}", copies, lambda nm=nm, at=at: getattr(k, nm).at[at, :, 1])

    def middle(self):
        k = self.k
        for s, (sec, _, width) in enumerate(CHUNKS):
            w = width / 256
            for j, nm, d, e in ((0, "X", R, L), (1, "D", L, R)):
                self.task(
                    f"m{s}{j}",
                    self.hands[nm, sec],
                    [*self.has[nm, sec], f"t{j}"],
                    lambda s=s, j=j: k.partial(s, j),
                    [
                        (f"r{s}{d}", ("x", d), w / 2,
                         lambda s=s, j=j: (k.at("PB", s).at[j, k.rows("far")], k.at("RL", s).at[j])),
                        (f"f{s}{j}{e}", ("x", e), w / 2,
                         lambda s=s, j=j, e=e: (k.at("PB", s).at[j, k.rows(e)], k.at("FN", s).at[e, j])),
                    ],
                )
                self.task(
                    f"l{s}{j}",
                    [f"r{s}{d}"],
                    [f"m{s}{j}"],
                    lambda s=s, j=j, d=d: k.relay(s, j, d),
                    [
                        (f"f{s}{j}{d}", ("x", d), w / 2,
                         lambda s=s, j=j, d=d: (k.at("PB", s).at[j, k.rows(d)], k.at("FN", s).at[d, j])),
                    ],
                )
            self.group(
                f"f{s}",
                [f"f{s}{j}{d}" for j in range(2) for d in (R, L)],
                lambda s=s: k.at("FN", s),
            )
            for j in range(2):
                self.group(
                    f"h{s}{j}",
                    [f"h{s}{j}{R}", f"h{s}{j}{L}"],
                    lambda s=s, j=j: k.at("AGB", s).at[j, k.rows("far")],
                )

            def mine(s=s, j=1):
                return (k.at("AGB", s).at[j, k.rows("own")],) * 2

            self.task(
                f"g{s}",
                [f"f{s}{j}{d}" for j in range(2) for d in (R, L)],
                [f"m{s}0", f"m{s}1"],
                lambda s=s: k.gelu(s),
                [(f"a{s}1{d}", ("x", d), w / 2, mine) for d in (R, L)],
            )
            self.task(
                f"u{s}",
                (),
                [f"g{s}"],
                None,
                [(f"a{s}0{d}", ("x", d), w / 2, lambda s=s: mine(s, 0)) for d in (R, L)],
            )
            for j, before in ((1, f"g{s}"), (0, f"u{s}")):
                for d, e in ((R, L), (L, R)):
                    self.task(
                        f"h{s}{j}{d}",
                        [f"a{s}{j}{d}"],
                        [before],
                        None,
                        [
                            (f"h{s}{j}{d}", ("x", d), w / 4,
                             lambda s=s, j=j, d=d, e=e: (k.at("AGB", s).at[j, k.rows(e, d)],) * 2),
                        ],
                    )

    def input_grad(self):
        k = self.k

        def first(s, q, d):
            return 0 if (s + q) % 2 == d else 1

        def start_slot(s, q, d):
            return SUM_SRC[d][first(s, q, d)]

        def half(q):
            return slice(96 * q, 96 * q + 96)

        def zsend(s, q, d, j):
            return (f"S{s}{q}{d}{j}", ("z", d), CHUNKS[s][2] / 512,
                    lambda: (k.at("IGP", s).at[SUM_SRC[d][j], 0, half(q)], k.at("ZR", s).at[d, j, half(q)]))

        def starts(s, q, p):
            return [zsend(s, q, d, first(s, q, d)) for d in (R, L) if start_slot(s, q, d) // 2 == p]

        late = {q for _, q in Y_FIRST}
        for s in range(len(CHUNKS)):
            for p in (3, 2, 1, 0):
                pair = slice(2 * p, 2 * p + 2)
                self.task(
                    f"i{s}{p}",
                    [f"a{s}1{R}", f"a{s}1{L}", f"h{s}1{R}", f"h{s}1{L}"],
                    [f"h{s}1{R}", f"h{s}1{L}"],
                    lambda s=s, p=p: k.ig_part(s, p),
                    [(f"C{s}{p}", ("p", 0), CHUNKS[s][2] / 128,
                      lambda s=s, pair=pair: (k.at("IGP", s).at[pair, 1], k.at("CR", s).at[pair]))],
                )
                sends = []
                for q in range(2):
                    if (s, q) in Y_FIRST:
                        sends.append((f"A{s}{q}{p}", ("y", s - 1), 1,
                                      lambda s=s, q=q, pair=pair: (k.at("IGP", s).at[pair, 0, half(q)],
                                                                   k.YA.at[s - 1, pair, half(q)])))
                    elif s > 0 or q not in late:
                        sends += starts(s, q, p)
                self.task(
                    f"c{s}{p}", [f"C{s}{p}"], [f"i{s}{p}"], lambda s=s, p=p: k.core_sum(s, p), sends
                )
                for q in sorted(late):
                    if s == 0:
                        froms = [t for t in (1, 2) if (t, q) in Y_FIRST]
                        self.task(
                            f"y{q}{p}",
                            [f"A{t}{q}{p}" for t in froms],
                            [f"c0{p}"] + [f"c{t}{p}" for t in froms],
                            lambda p=p, q=q, froms=froms: k.y_sum(p, half(q), froms),
                            starts(0, q, p),
                        )
        finals = {0: [], 1: []}
        for s in range(len(CHUNKS)):
            for q in range(2):
                if (s, q) in Y_FIRST:
                    continue

                def ready(slot, s=s, q=q):
                    return f"y{q}{slot // 2}" if s == 0 and q in late else f"c{s}{slot // 2}"

                for d in (R, L):
                    for j in range(first(s, q, d), 3):
                        self.task(
                            f"z{s}{q}{d}{j}",
                            [f"S{s}{q}{d}{j}"],
                            [ready(SUM_DST[d][j]), ready(start_slot(s, q, d))],
                            lambda s=s, q=q, d=d, j=j: k.z_sum(s, half(q), d, j),
                            [zsend(s, q, d, j + 1)],
                        )
                sends = []
                if s > 0:
                    link = ("y", (R, L, "far")[CHUNKS[s][0] - 1])
                    finals[q].append(f"F{s}{q}")
                    sends = [(f"F{s}{q}", link, CHUNKS[s][2] / 512,
                              lambda s=s, q=q: (k.at("IGP", s).at[0, 0, half(q)], k.at("YF", s).at[half(q)]))]
                self.task(
                    f"e{s}{q}",
                    [f"S{s}{q}{d}3" for d in (R, L)],
                    [f"z{s}{q}{d}2" for d in (R, L)] + [ready(0)],
                    lambda s=s, q=q: k.z_end(s, half(q)),
                    sends,
                )
        for q in range(2):
            froms = [int(n[1]) for n in finals[q]]
            self.task(
                f"end{q}",
                finals[q],
                [f"e0{q}"] + [f"e{t}{q}" for t in froms],
                lambda q=q, froms=froms: k.end(half(q), froms),
            )

    def weight_grads(self):
        k = self.k
        for s in range(len(CHUNKS)):
            for j in range(2):
                self.task(
                    f"v{s}{j}",
                    [f"a{s}{j}{R}", f"a{s}{j}{L}", f"h{s}{j}{R}", f"h{s}{j}{L}"],
                    [f"h{s}{j}{R}", f"h{s}{j}{L}"],
                    lambda s=s, j=j: k.turn_act(s, j),
                )
        for which, j in ((0, 1), (1, 0)):
            for slot in range(8):
                self.task(
                    f"w{which}{slot}",
                    (),
                    [f"v{s}{j}" for s in range(len(CHUNKS))] + ["t1"],
                    lambda which=which, slot=slot: k.weight_grad(which, slot),
                )


class Device:
    def __init__(self, **refs):
        self.__dict__.update(refs)

    def at(self, name, chunk):
        i = BUFS.index(name)
        return self.wide[i].at[chunk] if chunk < WIDE else self.narrow[i].at[chunk - WIDE]

    def block_rows(self, slot, other):
        row = turn(self.z, Z_REL[slot], self.n_z) * 2 + (1 - self.core if other else self.core)
        return pl.ds(pl.multiple_of(row * 192, 192), 192)

    def load(self):
        self.own = [
            pltpu.make_async_copy(a, b.at[0, 0, 0], self.local_sems.at[i])
            for i, (a, b) in enumerate(((self.x_in, self.X), (self.d_in, self.D)))
        ]
        for copy in self.own:
            copy.start()
        for i, src in enumerate((self.wu_in, self.wd_in)):
            for slot in range(8):
                for other in range(2):
                    rows = pl.ds((slot * 2 + other) * 192, 192)
                    dst = self.WU.at[slot, other] if i == 0 else self.gd_out.at[rows]
                    pltpu.make_async_copy(
                        src.at[self.block_rows(slot, other)], dst, self.local_sems.at[2 + i]
                    ).start()

    def own_wait(self):
        for copy in self.own:
            copy.wait()

    def transpose(self, j):
        src, dst = ((self.WU, self.UT), (self.gd_out, self.DT))[j]
        pltpu.make_async_copy(src, src, self.local_sems.at[2 + j]).wait()

        @pl.loop(0, 4)
        def _(p):
            if j == 0:
                dst[p] = src[pl.ds(p * 2, 2)].reshape(768, 384).T
            else:
                dst[p] = src[pl.ds(pl.multiple_of(p * 768, 768), 768)].T

    def rows(self, which, part=None):
        by = {R: 1, L: -1, "far": 2, "own": 0}[which]
        at = turn(self.c, by, self.n_col) * 96
        if part is None:
            return pl.ds(pl.multiple_of(at, 96), 96)
        return pl.ds(pl.multiple_of(at + 48 * part, 48), 48)

    def partial(self, s, j):
        b, w = ((self.X, self.UT), (self.D, self.DT))[j]
        sec, lane, width = CHUNKS[s]
        acc = jnp.zeros((384, width), f32)
        for p in range(4):
            tokens = b[sec, 2 * p : 2 * p + 2, :, :, lane : lane + width].reshape(768, width)
            acc += jnp.dot(w[p], tokens, preferred_element_type=f32)
        self.at("PB", s)[j] = acc.astype(bf16)

    def relay(self, s, j, d):
        rows = self.rows(d)
        self.at("PB", s)[j, rows] = (
            self.at("PB", s)[j, rows].astype(f32) + self.at("RL", s)[j].astype(f32)
        ).astype(bf16)

    def gelu(self, s):
        rows = self.rows("own")
        pre, back = (
            self.at("PB", s)[j, rows].astype(f32)
            + self.at("FN", s)[0, j].astype(f32)
            + self.at("FN", s)[1, j].astype(f32)
            for j in range(2)
        )
        act, grad = gelu_pair(pre, back)
        self.at("AGB", s)[0, rows] = act.astype(bf16)
        self.at("AGB", s)[1, rows] = grad.astype(bf16)

    def ig_part(self, s, p):
        w = self.WU[2 * p : 2 * p + 2].reshape(768, 384)
        g = jnp.dot(w, self.at("AGB", s)[1], preferred_element_type=f32)
        self.at("IGP", s)[2 * p : 2 * p + 2] = g.astype(bf16).reshape(2, 2, 192, CHUNKS[s][2])

    def core_sum(self, s, p):
        pair = slice(2 * p, 2 * p + 2)
        self.at("IGP", s)[pair, 0] = (
            self.at("IGP", s)[pair, 0].astype(f32) + self.at("CR", s)[pair].astype(f32)
        ).astype(bf16)

    def y_sum(self, p, rows, froms):
        pair = slice(2 * p, 2 * p + 2)
        total = self.at("IGP", 0)[pair, 0, rows].astype(f32)
        for t in froms:
            total += self.YA[t - 1, pair, rows].astype(f32)
        self.at("IGP", 0)[pair, 0, rows] = total.astype(bf16)

    def z_sum(self, s, rows, d, j):
        slot = SUM_DST[d][j]
        self.at("IGP", s)[slot, 0, rows] = (
            self.at("IGP", s)[slot, 0, rows].astype(f32) + self.at("ZR", s)[d, j, rows].astype(f32)
        ).astype(bf16)

    def z_end(self, s, rows):
        total = (
            self.at("IGP", s)[0, 0, rows].astype(f32)
            + self.at("ZR", s)[0, 3, rows].astype(f32)
            + self.at("ZR", s)[1, 3, rows].astype(f32)
        )
        if s == 0:
            self.ig_out[rows] = total
        else:
            self.at("IGP", s)[0, 0, rows] = total.astype(bf16)

    def end(self, rows, froms):
        for t in froms:
            lanes = slice(CHUNKS[t][1], CHUNKS[t][1] + CHUNKS[t][2])
            self.ig_out[rows, lanes] = self.ig_out[rows, lanes] + self.at("YF", t)[rows].astype(f32)

    def turn_act(self, s, j):
        sec, lane, width = CHUNKS[s]
        self.AT[j, sec, lane : lane + width] = self.at("AGB", s)[j].T

    def weight_grad(self, which, slot):
        b, j, out = ((self.X, 1, self.gu_out), (self.D, 0, self.gd_out))[which]
        acc = jnp.zeros((384, 384), f32)
        for s in range(4):
            acc += jnp.dot(
                b[s, slot].reshape(384, 256), self.AT[j, s], preferred_element_type=f32
            )
        acc = acc.astype(bf16)
        out[self.block_rows(slot, 0), :] = acc[:192]
        out[self.block_rows(slot, 1), :] = acc[192:]


def turn(i, by, n):
    return lax.rem(i + (by + n), n)


ORDER = (
    0, 1, 3, 7, 11, 14, 18, 21, 25, 8, 12, 15, 4, 22, 19, 2, 13, 9, 16, 29, 5, 23, 33, 36, 26,
    20, 10, 17, 27, 57, 43, 30, 24, 28, 58, 59, 40, 66, 34, 47, 68, 31, 60, 37, 44, 41, 48, 6,
    67, 69, 35, 76, 38, 32, 39, 45, 86, 42, 49, 78, 62, 53, 70, 51, 55, 46, 50, 63, 61, 71, 77,
    79, 65, 88, 54, 64, 72, 73, 52, 56, 96, 87, 98, 89, 80, 173, 97, 110, 74, 99, 90, 82, 106,
    83, 118, 100, 114, 93, 92, 101, 122, 124, 175, 126, 111, 102, 103, 91, 81, 130, 134, 132,
    177, 123, 131, 138, 104, 140, 75, 119, 107, 95, 125, 139, 105, 179, 182, 133, 141, 136, 135,
    84, 108, 142, 127, 160, 164, 85, 109, 178, 180, 115, 167, 143, 172, 158, 137, 181, 112, 94,
    146, 128, 161, 165, 144, 154, 149, 113, 174, 185, 129, 145, 159, 168, 176, 116, 147, 184,
    162, 191, 166, 155, 189, 117, 152, 150, 193, 186, 195, 163, 120, 148, 169, 194, 156, 121,
    153, 183, 187, 190, 192, 188, 151, 170, 157, 171,
)


def kernel(
    x_in, d_in, wu_in, wd_in,
    ig_out, gu_out, gd_out,
    X, D, WU, UT, DT, AT, YA,
    send_sems, recv_sems, local_sems,
    *chunk_bufs,
):
    refs = dict(locals())
    n_sec, n_row, n_col = (lax.axis_size(a) for a in ("section", "row", "col"))
    n_z = n_row // 2
    s, r, c = (lax.axis_index(a) for a in ("section", "row", "col"))
    z, core = r // 2, r % 2
    device_of = {("p", 0): {"row": z * 2 + (1 - core)}, ("y", "far"): {"section": turn(s, 2, n_sec)}}
    for d, by in ((R, 1), (L, -1)):
        device_of["z", d] = {"row": turn(z, by, n_z) * 2 + core}
        device_of["y", d] = {"section": turn(s, by, n_sec)}
        device_of["x", d] = {"col": turn(c, by, n_col)}

    barrier = pltpu.get_barrier_semaphore()
    for dev in device_of.values():
        pl.semaphore_signal(barrier, inc=1, device_id=dev, device_id_type=pl.DeviceIdType.MESH)
    here = Device(**refs, wide=chunk_bufs[: len(BUFS)], narrow=chunk_bufs[len(BUFS) :], z=z, core=core, c=c, n_z=n_z, n_col=n_col)
    here.load()
    pl.semaphore_wait(barrier, len(device_of))

    plan = Plan(here)
    tasks, groups = plan.tasks, plan.groups
    started, descriptors, arrived, done, recv_of = {}, [], set(), set(), {}
    names = list(tasks)
    assert sorted(ORDER) == list(range(len(names)))
    for name in (names[i] for i in ORDER):
        needs, after, do, sends = tasks[name]
        assert done.issuperset(after)
        for copy in needs:
            key = groups.get(copy, copy)
            if key not in arrived:
                arrived.add(key)
                if key in plan.regions:
                    region = plan.regions[key]()
                    pltpu.make_async_copy(region, region, recv_sems.at[recv_of[key]]).wait()
                else:
                    started[copy].wait_recv()
        if do is not None:
            do()
        for copy, link, _, of in sends:
            src, dst = of()
            i = len(descriptors)
            if i >= SEND_SEMS:
                descriptors[i - SEND_SEMS].wait_send()
            started[copy] = pltpu.make_async_remote_copy(
                src_ref=src,
                dst_ref=dst,
                send_sem=send_sems.at[i % SEND_SEMS],
                recv_sem=recv_sems.at[recv_of.setdefault(groups.get(copy, copy), len(recv_of))],
                device_id=device_of[link],
                device_id_type=pl.DeviceIdType.MESH,
            )
            started[copy].start()
            descriptors.append(started[copy])
        done.add(name)
    assert arrived == set(recv_of) and len(recv_of) <= RECV_SEMS
    for copy in descriptors[-SEND_SEMS:]:
        copy.wait_send()


def chunk_buffers(n, width):
    shapes = (
        (2, 384),
        (2, 96),
        (2, 2, 96),
        (2, 384),
        (8, 2, 192),
        (8, 192),
        (2, 4, 192),
        (192,),
    )
    return [pltpu.VMEM((n, *shape, width), bf16) for shape in shapes]


def on_device(inputs, out_grad, w_up, w_down):
    any_spec = pl.BlockSpec(memory_space=pl.ANY)
    ig_t, gu, gd = pl.pallas_call(
        kernel,
        out_shape=(
            pltpu.VMEM((192, 256), f32),
            pltpu.VMEM((3072, 384), bf16),
            pltpu.VMEM((3072, 384), bf16),
        ),
        in_specs=[any_spec] * 4,
        out_specs=(pl.BlockSpec(memory_space=pltpu.VMEM),) * 3,
        scratch_shapes=[
            pltpu.VMEM((4, 8, 2, 192, 256), bf16),
            pltpu.VMEM((4, 8, 2, 192, 256), bf16),
            pltpu.VMEM((8, 2, 192, 384), bf16),
            pltpu.VMEM((4, 384, 768), bf16),
            pltpu.VMEM((4, 384, 768), bf16),
            pltpu.VMEM((2, 4, 256, 384), bf16),
            pltpu.VMEM((2, 8, 192, 256), bf16),
            pltpu.SemaphoreType.DMA((SEND_SEMS,)),
            pltpu.SemaphoreType.DMA((RECV_SEMS,)),
            pltpu.SemaphoreType.DMA((4,)),
            *chunk_buffers(WIDE, 256),
            *(chunk_buffers(len(CHUNKS) - WIDE, 128) if len(CHUNKS) > WIDE else ()),
        ],
        compiler_params=pltpu.CompilerParams(
            collective_id=0, has_side_effects=True, vmem_limit_bytes=52 * 2**20
        ),
        cost_estimate=pl.CostEstimate(
            flops=5 * 2 * 1024 * 3072 * 384, bytes_accessed=10_000_000, transcendentals=98304
        ),
        name="ffn_backward",
    )(inputs.T, out_grad.T, w_up, w_down)
    return ig_t.T, gu, gd


def solution(mesh):
    return jax.shard_map(
        on_device,
        mesh=mesh,
        in_specs=(
            P("section", ("col", "row")),
            P("section", ("col", "row")),
            P("col", ("section", "row")),
            P("col", ("section", "row")),
        ),
        out_specs=(
            P("section", ("col", "row")),
            P("col", ("section", "row")),
            P("col", ("section", "row")),
        ),
        check_vma=False,
    )
```

```python
import functools

import jax
import jax.numpy as jnp
from jax import lax
from jax.experimental import pallas as pl
from jax.experimental.pallas import tpu as pltpu
from jax.sharding import PartitionSpec as P

coeff = 0.7978845608028654
f32 = jnp.float32
bf16 = jnp.bfloat16
R, L = 0, 1
SEND_SEMS = 48
RECV_SEMS = 153

Z_REL = (0, 1, -1, 2, -2, 3, -3, 4)
GATHER_SRC = {R: (0, 2, 4, 6), L: (0, 1, 3, 5)}
GATHER_DST = {R: (2, 4, 6, 7), L: (1, 3, 5, 7)}
GROUPS = {1: (0, 3), 2: (3, 5), 3: (5, 7), 4: (7, 8)}
SUM_SRC = {R: (7, 5, 3, 1), L: (7, 6, 4, 2)}
SUM_DST = {R: (5, 3, 1, 0), L: (6, 4, 2, 0)}
X_FAR = ((0, 3), (3, 7), (7, 8))
D_FAR = ((5, 6), (6, 8))
Y_FIRST = ((1, 0), (2, 0), (1, 1), (2, 1))
CHUNKS = ((0, 0, 256), (1, 0, 256), (2, 0, 256), (3, 0, 256))
WIDE = 4
DIRECT = (0, 1, 2, 3)
BUFS = ("PB", "RL", "FN", "AGB", "IGP", "CR", "ZR", "YF")


def gelu_pair(pre, back):
    inner = coeff * (pre + 0.044715 * pre * pre * pre)
    tanh_val = jnp.tanh(inner)
    act = 0.5 * pre * (1.0 + tanh_val)
    slope = 0.5 * (1.0 + tanh_val) + 0.5 * pre * (1.0 - tanh_val * tanh_val) * coeff * (
        1.0 + 3.0 * 0.044715 * pre * pre
    )
    return act, back * slope


class Plan:
    def __init__(self, k):
        self.k = k
        self.tasks = {}
        self.groups = {}
        self.regions = {}
        self.gather()
        self.middle()
        self.input_grad()
        self.weight_grads()

    def group(self, name, copies, region):
        self.groups.update({copy: name for copy in copies})
        self.regions[name] = region

    def task(self, name, needs=(), after=(), do=None, sends=()):
        assert name not in self.tasks
        self.tasks[name] = (tuple(needs), tuple(after), do, tuple(sends))

    def gather(self):
        k = self.k
        last = {("X", 0): (4, 3), ("D", 0): (3, 4), ("D", 1): (4, 3), ("D", 2): (3, 4), ("D", 3): (2, 2)}

        def hop(nm, sec, h, d):
            link = ("z", d)

            def refs():
                b = getattr(k, nm)
                src = b.at[sec, GATHER_SRC[d][h - 1], 0]
                if sec == 0 and h == 1:
                    src = k.x_in if nm == "X" else k.d_in
                return src, b.at[sec, GATHER_DST[d][h - 1], 0]

            return (f"{nm}{sec}z{h}{d}", link, 1, refs)

        def move(name, link, nm, sec, to, lo, hi, half=(0, 0)):
            def refs():
                b = getattr(k, nm)
                return b.at[sec, lo:hi, half[0]], b.at[to, lo:hi, half[1]]

            n = (hi - lo) * (2 if isinstance(sec, slice) else 1)
            return (name, link, n, refs)

        def hand(nm, sec, tag, lo, hi):
            return move(f"{nm}{sec}c{tag}", ("p", 0), nm, sec, sec, lo, hi, (0, 1))

        self.task(
            "go",
            sends=[hop(nm, 0, 1, d) for nm in "XD" for d in (R, L)]
            + [
                ("DyR", ("y", R), 1, lambda: (k.d_in, k.D.at[2, 0, 0])),
                ("DyL", ("y", L), 1, lambda: (k.d_in, k.D.at[1, 0, 0])),
            ],
        )
        self.task("own", after=["go"], do=lambda: k.own_wait())
        for j in range(2):
            self.task(f"t{j}", after=["own"], do=lambda j=j: k.transpose(j))
        self.task("D1s", ["DyL"], ["own"], sends=[hop("D", 1, 1, d) for d in (R, L)])
        self.task(
            "D2s",
            ["DyR"],
            ["own"],
            sends=[
                ("Dy2", ("y", R), 1, lambda: (k.D.at[2, 0, 0], k.D.at[3, 0, 0])),
                *(hop("D", 2, 1, d) for d in (R, L)),
            ],
        )
        self.task("D3s", ["Dy2"], ["own"], sends=[hop("D", 3, 1, d) for d in (R, L)])
        for (nm, sec), hops in last.items():
            for d in (R, L):
                for h in range(1, hops[d] + 1):
                    more = [hop(nm, sec, h + 1, d)] if h < hops[d] else []
                    self.task(f"{nm}{sec}z{h}{d}", [f"{nm}{sec}z{h}{d}"], ["own"], sends=more)
            for h, (lo, hi) in GROUPS.items():
                got = [f"{nm}{sec}z{h}{d}" for d in (R, L) if h <= hops[d]]
                if not got:
                    continue
                sends = []
                if nm == "X":
                    sends.append(move(f"Xy{h}{R}", ("y", R), "X", 0, 2, lo, hi))
                    sends.append(move(f"Xy{h}{L}", ("y", L), "X", 0, 1, lo, hi))
                sends.append(hand(nm, sec, h, lo, hi))
                if nm == "D" and sec == 2 and h == 3:
                    sends.insert(0, move("Df0", ("y", R), "D", 2, 3, *D_FAR[0]))
                if nm == "D" and sec == 1 and h == 4:
                    got.append("D1g3")
                    sends.insert(0, move("Df1", ("y", L), "D", 1, 3, *D_FAR[1]))
                if nm == "D" and sec > 0:
                    got.append(f"D{sec}s")
                self.task(f"{nm}{sec}g{h}", after=got, sends=sends)
        for h, (lo, hi) in GROUPS.items():
            sends = []
            if h == 1:
                sends.append(move("Xf0", ("y", R), "X", 2, 3, *X_FAR[0]))
            if h == 3:
                sends.append(move("Xf1", ("y", L), "X", 1, 3, *X_FAR[1]))
            if h == 4:
                sends.append(move("Xf2", ("y", R), "X", 2, 3, *X_FAR[2]))
            sends.append(move(f"Xyc{h}", ("p", 0), "X", slice(1, 3), slice(1, 3), lo, hi, (0, 1)))
            prior = ["own"] if h == 1 else [f"Xy{h - 1}"]
            self.task(f"Xy{h}", [f"Xy{h}{R}", f"Xy{h}{L}"], prior, sends=sends)
        for nm, far in (("X", X_FAR), ("D", D_FAR)):
            for i, (lo, hi) in enumerate(far):
                self.task(
                    f"{nm}f{i}", [f"{nm}f{i}"], ["own"], sends=[hand(nm, 3, f"f{i}", lo, hi)]
                )
        self.has = {
            (nm, sec): [
                *(f"{nm}{sec}g{h}" for h in GROUPS if f"{nm}{sec}g{h}" in self.tasks),
                *((f"{nm}f{i}" for i in range(len(far))) if sec == 3 else ()),
                *((f"Xy{h}" for h in GROUPS) if nm == "X" and sec in (1, 2) else ()),
            ]
            for nm, far in (("X", X_FAR), ("D", D_FAR))
            for sec in range(4)
        }
        self.hands = {}
        for (nm, sec), names in self.has.items():
            copies = []
            for n in names:
                copies += [c[0] for c in self.tasks[n][3] if c[1][0] == "p"]
            self.hands[nm, sec] = copies
            at = slice(1, 3) if nm == "X" and sec in (1, 2) else sec
            self.group(f"{nm}{at}", copies, lambda nm=nm, at=at: getattr(k, nm).at[at, :, 1])

    def middle(self):
        k = self.k
        for s, (sec, _, width) in enumerate(CHUNKS):
            w = width / 256
            for j, nm, d, e in ((0, "X", R, L), (1, "D", L, R)):
                self.task(
                    f"m{s}{j}",
                    self.hands[nm, sec],
                    [*self.has[nm, sec], f"t{j}"],
                    lambda s=s, j=j: k.partial(s, j),
                    [
                        (f"r{s}{d}", ("x", d), w / 2,
                         lambda s=s, j=j: (k.at("PB", s).at[j, k.rows("far")], k.at("RL", s).at[j])),
                        (f"f{s}{j}{e}", ("x", e), w / 2,
                         lambda s=s, j=j, e=e: (k.at("PB", s).at[j, k.rows(e)], k.at("FN", s).at[e, j])),
                    ],
                )
                self.task(
                    f"l{s}{j}",
                    [f"r{s}{d}"],
                    [f"m{s}{j}"],
                    lambda s=s, j=j, d=d: k.relay(s, j, d),
                    [
                        (f"f{s}{j}{d}", ("x", d), w / 2,
                         lambda s=s, j=j, d=d: (k.at("PB", s).at[j, k.rows(d)], k.at("FN", s).at[d, j])),
                    ],
                )
            self.group(
                f"f{s}",
                [f"f{s}{j}{d}" for j in range(2) for d in (R, L)],
                lambda s=s: k.at("FN", s),
            )
            for j in range(2):
                if j == 1 and s in DIRECT:
                    continue
                self.group(
                    f"h{s}{j}",
                    [f"h{s}{j}{R}", f"h{s}{j}{L}"],
                    lambda s=s, j=j: k.at("AGB", s).at[j, k.rows("far")],
                )

            def mine(s=s, j=1):
                return (k.at("AGB", s).at[j, k.rows("own")],) * 2

            self.task(
                f"g{s}",
                [f"f{s}{j}{d}" for j in range(2) for d in (R, L)],
                [f"m{s}0", f"m{s}1"],
                lambda s=s: k.gelu(s),
                [(f"a{s}1{d}", ("x", d), w / 2, mine)
                 for d in ((*(("far",) if s in DIRECT else ()), R, L))],
            )
            self.task(
                f"u{s}",
                (),
                [f"g{s}"],
                None,
                [(f"a{s}0{d}", ("x", d), w / 2, lambda s=s: mine(s, 0)) for d in (R, L)],
            )
            for j, before in ((1, f"g{s}"), (0, f"u{s}")):
                for d, e in ((R, L), (L, R)):
                    if j == 1 and s in DIRECT:
                        continue
                    self.task(
                        f"h{s}{j}{d}",
                        [f"a{s}{j}{d}"],
                        [before],
                        None,
                        [
                            (f"h{s}{j}{d}", ("x", d), w / 4,
                             lambda s=s, j=j, d=d, e=e: (k.at("AGB", s).at[j, k.rows(e, d)],) * 2),
                        ],
                    )

    def spread(self, s, j):
        copies = [f"a{s}{j}{d}" for d in (R, L)]
        if j == 1 and s in DIRECT:
            return [*copies, f"a{s}1far"], [f"g{s}"]
        relays = [f"h{s}{j}{d}" for d in (R, L)]
        return copies + relays, relays

    def input_grad(self):
        k = self.k

        def first(s, q, d):
            return 0 if (s + q) % 2 == d else 1

        def start_slot(s, q, d):
            return SUM_SRC[d][first(s, q, d)]

        def half(q):
            return slice(96 * q, 96 * q + 96)

        def zsend(s, q, d, j):
            return (f"S{s}{q}{d}{j}", ("z", d), CHUNKS[s][2] / 512,
                    lambda: (k.at("IGP", s).at[SUM_SRC[d][j], 0, half(q)], k.at("ZR", s).at[d, j, half(q)]))

        def starts(s, q, p):
            return [zsend(s, q, d, first(s, q, d)) for d in (R, L) if start_slot(s, q, d) // 2 == p]

        late = {q for _, q in Y_FIRST}
        for s in range(len(CHUNKS)):
            for p in (3, 2, 1, 0):
                pair = slice(2 * p, 2 * p + 2)
                self.task(
                    f"i{s}{p}",
                    *self.spread(s, 1),
                    lambda s=s, p=p: k.ig_part(s, p),
                    [(f"C{s}{p}", ("p", 0), CHUNKS[s][2] / 128,
                      lambda s=s, pair=pair: (k.at("IGP", s).at[pair, 1], k.at("CR", s).at[pair]))],
                )
                sends = []
                for q in range(2):
                    if (s, q) in Y_FIRST:
                        sends.append((f"A{s}{q}{p}", ("y", s - 1), 1,
                                      lambda s=s, q=q, pair=pair: (k.at("IGP", s).at[pair, 0, half(q)],
                                                                   k.YA.at[s - 1, pair, half(q)])))
                    elif s > 0 or q not in late:
                        sends += starts(s, q, p)
                self.task(
                    f"c{s}{p}", [f"C{s}{p}"], [f"i{s}{p}"], lambda s=s, p=p: k.core_sum(s, p), sends
                )
                for q in sorted(late):
                    if s == 0:
                        froms = [t for t in (1, 2) if (t, q) in Y_FIRST]
                        self.task(
                            f"y{q}{p}",
                            [f"A{t}{q}{p}" for t in froms],
                            [f"c0{p}"] + [f"c{t}{p}" for t in froms],
                            lambda p=p, q=q, froms=froms: k.y_sum(p, half(q), froms),
                            starts(0, q, p),
                        )
        finals = {0: [], 1: []}
        for s in range(len(CHUNKS)):
            for q in range(2):
                if (s, q) in Y_FIRST:
                    continue

                def ready(slot, s=s, q=q):
                    return f"y{q}{slot // 2}" if s == 0 and q in late else f"c{s}{slot // 2}"

                for d in (R, L):
                    for j in range(first(s, q, d), 3):
                        self.task(
                            f"z{s}{q}{d}{j}",
                            [f"S{s}{q}{d}{j}"],
                            [ready(SUM_DST[d][j]), ready(start_slot(s, q, d))],
                            lambda s=s, q=q, d=d, j=j: k.z_sum(s, half(q), d, j),
                            [zsend(s, q, d, j + 1)],
                        )
                sends = []
                if s > 0:
                    link = ("y", (R, L, "far")[CHUNKS[s][0] - 1])
                    finals[q].append(f"F{s}{q}")
                    sends = [(f"F{s}{q}", link, CHUNKS[s][2] / 512,
                              lambda s=s, q=q: (k.at("IGP", s).at[0, 0, half(q)], k.at("YF", s).at[half(q)]))]
                self.task(
                    f"e{s}{q}",
                    [f"S{s}{q}{d}3" for d in (R, L)],
                    [f"z{s}{q}{d}2" for d in (R, L)] + [ready(0)],
                    lambda s=s, q=q: k.z_end(s, half(q)),
                    sends,
                )
        for q in range(2):
            froms = [int(n[1]) for n in finals[q]]
            self.task(
                f"end{q}",
                finals[q],
                [f"e0{q}"] + [f"e{t}{q}" for t in froms],
                lambda q=q, froms=froms: k.end(half(q), froms),
            )

    def weight_grads(self):
        k = self.k
        for s in range(len(CHUNKS)):
            for j in range(2):
                self.task(
                    f"v{s}{j}",
                    *self.spread(s, j),
                    lambda s=s, j=j: k.turn_act(s, j),
                )
        for which, j in ((0, 1), (1, 0)):
            for slot in range(8):
                self.task(
                    f"w{which}{slot}",
                    (),
                    [f"v{s}{j}" for s in range(len(CHUNKS))] + ["t1"],
                    lambda which=which, slot=slot: k.weight_grad(which, slot),
                )


class Device:
    def __init__(self, **refs):
        self.__dict__.update(refs)

    def at(self, name, chunk):
        i = BUFS.index(name)
        return self.wide[i].at[chunk] if chunk < WIDE else self.narrow[i].at[chunk - WIDE]

    def block_rows(self, slot, other):
        row = turn(self.z, Z_REL[slot], self.n_z) * 2 + (1 - self.core if other else self.core)
        return pl.ds(pl.multiple_of(row * 192, 192), 192)

    def load(self):
        self.own = [
            pltpu.make_async_copy(a, b.at[0, 0, 0], self.local_sems.at[i])
            for i, (a, b) in enumerate(((self.x_in, self.X), (self.d_in, self.D)))
        ]
        for copy in self.own:
            copy.start()
        for i, src in enumerate((self.wu_in, self.wd_in)):
            for slot in range(8):
                for other in range(2):
                    rows = pl.ds((slot * 2 + other) * 192, 192)
                    dst = self.WU.at[slot, other] if i == 0 else self.gd_out.at[rows]
                    pltpu.make_async_copy(
                        src.at[self.block_rows(slot, other)], dst, self.local_sems.at[2 + i]
                    ).start()

    def own_wait(self):
        for copy in self.own:
            copy.wait()

    def transpose(self, j):
        src, dst = ((self.WU, self.UT), (self.gd_out, self.DT))[j]
        pltpu.make_async_copy(src, src, self.local_sems.at[2 + j]).wait()

        @pl.loop(0, 4)
        def _(p):
            if j == 0:
                dst[p] = src[pl.ds(p * 2, 2)].reshape(768, 384).T
            else:
                dst[p] = src[pl.ds(pl.multiple_of(p * 768, 768), 768)].T

    def rows(self, which, part=None):
        by = {R: 1, L: -1, "far": 2, "own": 0}[which]
        at = turn(self.c, by, self.n_col) * 96
        if part is None:
            return pl.ds(pl.multiple_of(at, 96), 96)
        return pl.ds(pl.multiple_of(at + 48 * part, 48), 48)

    def partial(self, s, j):
        b, w = ((self.X, self.UT), (self.D, self.DT))[j]
        sec, lane, width = CHUNKS[s]
        acc = jnp.zeros((384, width), f32)
        for p in range(4):
            tokens = b[sec, 2 * p : 2 * p + 2, :, :, lane : lane + width].reshape(768, width)
            acc += jnp.dot(w[p], tokens, preferred_element_type=f32)
        self.at("PB", s)[j] = acc.astype(bf16)

    def relay(self, s, j, d):
        rows = self.rows(d)
        self.at("PB", s)[j, rows] = (
            self.at("PB", s)[j, rows].astype(f32) + self.at("RL", s)[j].astype(f32)
        ).astype(bf16)

    def gelu(self, s):
        rows = self.rows("own")
        pre, back = (
            self.at("PB", s)[j, rows].astype(f32)
            + self.at("FN", s)[0, j].astype(f32)
            + self.at("FN", s)[1, j].astype(f32)
            for j in range(2)
        )
        act, grad = gelu_pair(pre, back)
        self.at("AGB", s)[0, rows] = act.astype(bf16)
        self.at("AGB", s)[1, rows] = grad.astype(bf16)

    def ig_part(self, s, p):
        w = self.WU[2 * p : 2 * p + 2].reshape(768, 384)
        g = jnp.dot(w, self.at("AGB", s)[1], preferred_element_type=f32)
        self.at("IGP", s)[2 * p : 2 * p + 2] = g.astype(bf16).reshape(2, 2, 192, CHUNKS[s][2])

    def core_sum(self, s, p):
        pair = slice(2 * p, 2 * p + 2)
        self.at("IGP", s)[pair, 0] = (
            self.at("IGP", s)[pair, 0].astype(f32) + self.at("CR", s)[pair].astype(f32)
        ).astype(bf16)

    def y_sum(self, p, rows, froms):
        pair = slice(2 * p, 2 * p + 2)
        total = self.at("IGP", 0)[pair, 0, rows].astype(f32)
        for t in froms:
            total += self.YA[t - 1, pair, rows].astype(f32)
        self.at("IGP", 0)[pair, 0, rows] = total.astype(bf16)

    def z_sum(self, s, rows, d, j):
        slot = SUM_DST[d][j]
        self.at("IGP", s)[slot, 0, rows] = (
            self.at("IGP", s)[slot, 0, rows].astype(f32) + self.at("ZR", s)[d, j, rows].astype(f32)
        ).astype(bf16)

    def z_end(self, s, rows):
        total = (
            self.at("IGP", s)[0, 0, rows].astype(f32)
            + self.at("ZR", s)[0, 3, rows].astype(f32)
            + self.at("ZR", s)[1, 3, rows].astype(f32)
        )
        if s == 0:
            self.ig_out[rows] = total
        else:
            self.at("IGP", s)[0, 0, rows] = total.astype(bf16)

    def end(self, rows, froms):
        for t in froms:
            lanes = slice(CHUNKS[t][1], CHUNKS[t][1] + CHUNKS[t][2])
            self.ig_out[rows, lanes] = self.ig_out[rows, lanes] + self.at("YF", t)[rows].astype(f32)

    def turn_act(self, s, j):
        sec, lane, width = CHUNKS[s]
        self.AT[j, sec, lane : lane + width] = self.at("AGB", s)[j].T

    def weight_grad(self, which, slot):
        b, j, out = ((self.X, 1, self.gu_out), (self.D, 0, self.gd_out))[which]
        acc = jnp.zeros((384, 384), f32)
        for s in range(4):
            acc += jnp.dot(
                b[s, slot].reshape(384, 256), self.AT[j, s], preferred_element_type=f32
            )
        acc = acc.astype(bf16)
        out[self.block_rows(slot, 0), :] = acc[:192]
        out[self.block_rows(slot, 1), :] = acc[192:]


def turn(i, by, n):
    return lax.rem(i + (by + n), n)


ORDER = (
    0, 1, 7, 11, 14, 18, 21, 25, 8, 12, 15, 4, 9, 22, 13, 16, 19, 2, 29, 26, 5, 23, 10, 17, 33,
    57, 58, 3, 43, 20, 27, 66, 30, 24, 28, 59, 40, 34, 37, 36, 68, 31, 60, 47, 67, 44, 6, 82,
    41, 69, 35, 38, 74, 32, 39, 45, 48, 61, 76, 51, 53, 55, 70, 42, 49, 75, 63, 46, 50, 62, 77,
    65, 84, 54, 52, 56, 83, 64, 90, 92, 98, 85, 78, 110, 106, 91, 102, 93, 165, 99, 86, 103,
    111, 167, 107, 116, 94, 118, 114, 71, 95, 79, 122, 126, 124, 115, 87, 123, 117, 130, 132,
    125, 136, 131, 73, 72, 171, 134, 133, 119, 128, 100, 169, 177, 127, 97, 152, 156, 101, 80,
    96, 120, 159, 135, 150, 174, 88, 89, 81, 104, 138, 141, 121, 176, 153, 157, 178, 146, 137,
    105, 151, 172, 129, 160, 166, 108, 139, 168, 173, 170, 154, 158, 179, 147, 109, 144, 164,
    180, 186, 175, 112, 140, 155, 142, 161, 148, 113, 145, 181, 187, 185, 184, 183, 182, 143,
    162, 149, 163,
)


def kernel(
    x_in, d_in, wu_in, wd_in,
    ig_out, gu_out, gd_out,
    X, D, WU, UT, DT, AT, YA,
    send_sems, recv_sems, local_sems,
    *chunk_bufs,
):
    refs = dict(locals())
    n_sec, n_row, n_col = (lax.axis_size(a) for a in ("section", "row", "col"))
    n_z = n_row // 2
    s, r, c = (lax.axis_index(a) for a in ("section", "row", "col"))
    z, core = r // 2, r % 2
    device_of = {("p", 0): {"row": z * 2 + (1 - core)}, ("y", "far"): {"section": turn(s, 2, n_sec)}}
    if DIRECT:
        device_of["x", "far"] = {"col": turn(c, 2, n_col)}
    for d, by in ((R, 1), (L, -1)):
        device_of["z", d] = {"row": turn(z, by, n_z) * 2 + core}
        device_of["y", d] = {"section": turn(s, by, n_sec)}
        device_of["x", d] = {"col": turn(c, by, n_col)}

    barrier = pltpu.get_barrier_semaphore()
    for dev in device_of.values():
        pl.semaphore_signal(barrier, inc=1, device_id=dev, device_id_type=pl.DeviceIdType.MESH)
    here = Device(**refs, wide=chunk_bufs[: len(BUFS)], narrow=chunk_bufs[len(BUFS) :], z=z, core=core, c=c, n_z=n_z, n_col=n_col)
    here.load()
    pl.semaphore_wait(barrier, len(device_of))

    plan = Plan(here)
    tasks, groups = plan.tasks, plan.groups
    started, descriptors, arrived, done, recv_of = {}, [], set(), set(), {}
    names = list(tasks)
    assert sorted(ORDER) == list(range(len(names)))
    for name in (names[i] for i in ORDER):
        needs, after, do, sends = tasks[name]
        assert done.issuperset(after)
        for copy in needs:
            key = groups.get(copy, copy)
            if key not in arrived:
                arrived.add(key)
                if key in plan.regions:
                    region = plan.regions[key]()
                    pltpu.make_async_copy(region, region, recv_sems.at[recv_of[key]]).wait()
                else:
                    started[copy].wait_recv()
        if do is not None:
            do()
        for copy, link, _, of in sends:
            src, dst = of()
            i = len(descriptors)
            if i >= SEND_SEMS:
                descriptors[i - SEND_SEMS].wait_send()
            started[copy] = pltpu.make_async_remote_copy(
                src_ref=src,
                dst_ref=dst,
                send_sem=send_sems.at[i % SEND_SEMS],
                recv_sem=recv_sems.at[recv_of.setdefault(groups.get(copy, copy), len(recv_of))],
                device_id=device_of[link],
                device_id_type=pl.DeviceIdType.MESH,
            )
            started[copy].start()
            descriptors.append(started[copy])
        done.add(name)
    assert arrived == set(recv_of) and len(recv_of) <= RECV_SEMS
    for copy in descriptors[-SEND_SEMS:]:
        copy.wait_send()


def chunk_buffers(n, width):
    shapes = (
        (2, 384),
        (2, 96),
        (2, 2, 96),
        (2, 384),
        (8, 2, 192),
        (8, 192),
        (2, 4, 192),
        (192,),
    )
    return [pltpu.VMEM((n, *shape, width), bf16) for shape in shapes]


def on_device(inputs, out_grad, w_up, w_down):
    any_spec = pl.BlockSpec(memory_space=pl.ANY)
    ig_t, gu, gd = pl.pallas_call(
        kernel,
        out_shape=(
            pltpu.VMEM((192, 256), f32),
            pltpu.VMEM((3072, 384), bf16),
            pltpu.VMEM((3072, 384), bf16),
        ),
        in_specs=[any_spec] * 4,
        out_specs=(pl.BlockSpec(memory_space=pltpu.VMEM),) * 3,
        scratch_shapes=[
            pltpu.VMEM((4, 8, 2, 192, 256), bf16),
            pltpu.VMEM((4, 8, 2, 192, 256), bf16),
            pltpu.VMEM((8, 2, 192, 384), bf16),
            pltpu.VMEM((4, 384, 768), bf16),
            pltpu.VMEM((4, 384, 768), bf16),
            pltpu.VMEM((2, 4, 256, 384), bf16),
            pltpu.VMEM((2, 8, 192, 256), bf16),
            pltpu.SemaphoreType.DMA((SEND_SEMS,)),
            pltpu.SemaphoreType.DMA((RECV_SEMS,)),
            pltpu.SemaphoreType.DMA((4,)),
            *chunk_buffers(WIDE, 256),
            *(chunk_buffers(len(CHUNKS) - WIDE, 128) if len(CHUNKS) > WIDE else ()),
        ],
        compiler_params=pltpu.CompilerParams(
            collective_id=0, has_side_effects=True, vmem_limit_bytes=52 * 2**20
        ),
        cost_estimate=pl.CostEstimate(
            flops=5 * 2 * 1024 * 3072 * 384, bytes_accessed=10_000_000, transcendentals=98304
        ),
        name="ffn_backward",
    )(inputs.T, out_grad.T, w_up, w_down)
    return ig_t.T, gu, gd


def solution(mesh):
    return jax.shard_map(
        on_device,
        mesh=mesh,
        in_specs=(
            P("section", ("col", "row")),
            P("section", ("col", "row")),
            P("col", ("section", "row")),
            P("col", ("section", "row")),
        ),
        out_specs=(
            P("section", ("col", "row")),
            P("col", ("section", "row")),
            P("col", ("section", "row")),
        ),
        check_vma=False,
    )
```

```python
import functools

import jax
import jax.numpy as jnp
from jax import lax
from jax.experimental import pallas as pl
from jax.experimental.pallas import tpu as pltpu
from jax.sharding import PartitionSpec as P

coeff = 0.7978845608028654
f32 = jnp.float32
bf16 = jnp.bfloat16
R, L = 0, 1
SEND_SEMS = 48
RECV_SEMS = 78

Z_REL = (0, 1, -1, 2, -2, 3, -3, 4)
GATHER_SRC = {R: (0, 2, 4, 6), L: (0, 1, 3, 5)}
GATHER_DST = {R: (2, 4, 6, 7), L: (1, 3, 5, 7)}
GROUPS = {1: (0, 3), 2: (3, 5), 3: (5, 7), 4: (7, 8)}
SUM_SRC = {R: (7, 5, 3, 1), L: (7, 6, 4, 2)}
SUM_DST = {R: (5, 3, 1, 0), L: (6, 4, 2, 0)}
X_FAR = ((0, 3), (3, 7), (7, 8))
D_FAR = ((5, 6), (6, 8))
Y_FIRST = ((1, 0), (2, 0), (1, 1), (2, 1))
CHUNKS = ((0, 0, 256), (1, 0, 256), (2, 0, 256), (3, 0, 256))
WIDE = 4
DIRECT = (0, 1, 2, 3)
BUFS = ("PB", "RL", "FN", "AGB", "IGP", "CR", "ZR", "YF")


def gelu_pair(pre, back):
    inner = coeff * (pre + 0.044715 * pre * pre * pre)
    tanh_val = jnp.tanh(inner)
    act = 0.5 * pre * (1.0 + tanh_val)
    slope = 0.5 * (1.0 + tanh_val) + 0.5 * pre * (1.0 - tanh_val * tanh_val) * coeff * (
        1.0 + 3.0 * 0.044715 * pre * pre
    )
    return act, back * slope


class Plan:
    def __init__(self, k):
        self.k = k
        self.tasks = {}
        self.groups = {}
        self.regions = {}
        self.gather()
        self.middle()
        self.input_grad()
        self.weight_grads()

    def group(self, name, copies, region):
        self.groups.update({copy: name for copy in copies})
        self.regions[name] = region

    def task(self, name, needs=(), after=(), do=None, sends=()):
        assert name not in self.tasks
        self.tasks[name] = (tuple(needs), tuple(after), do, tuple(sends))

    def gather(self):
        k = self.k
        last = {("X", 0): (4, 3), ("D", 0): (3, 4), ("D", 1): (4, 3), ("D", 2): (3, 4), ("D", 3): (2, 2)}

        def hop(nm, sec, h, d):
            link = ("z", d)

            def refs():
                b = getattr(k, nm)
                src = b.at[sec, GATHER_SRC[d][h - 1], 0]
                if sec == 0 and h == 1:
                    src = k.x_in if nm == "X" else k.d_in
                return src, b.at[sec, GATHER_DST[d][h - 1], 0]

            return (f"{nm}{sec}z{h}{d}", link, 1, refs)

        def move(name, link, nm, sec, to, lo, hi, half=(0, 0)):
            def refs():
                b = getattr(k, nm)
                return b.at[sec, lo:hi, half[0]], b.at[to, lo:hi, half[1]]

            n = (hi - lo) * (2 if isinstance(sec, slice) else 1)
            return (name, link, n, refs)

        def hand(nm, sec, tag, lo, hi):
            return move(f"{nm}{sec}c{tag}", ("p", 0), nm, sec, sec, lo, hi, (0, 1))

        self.task(
            "go",
            sends=[hop(nm, 0, 1, d) for nm in "XD" for d in (R, L)]
            + [
                ("DyR", ("y", R), 1, lambda: (k.d_in, k.D.at[2, 0, 0])),
                ("DyL", ("y", L), 1, lambda: (k.d_in, k.D.at[1, 0, 0])),
            ],
        )
        self.task("own", after=["go"], do=lambda: k.own_wait())
        for j in range(2):
            self.task(f"t{j}", after=["own"], do=lambda j=j: k.transpose(j))
        self.task("D1s", ["DyL"], ["own"], sends=[hop("D", 1, 1, d) for d in (R, L)])
        self.task(
            "D2s",
            ["DyR"],
            ["own"],
            sends=[
                ("Dy2", ("y", R), 1, lambda: (k.D.at[2, 0, 0], k.D.at[3, 0, 0])),
                *(hop("D", 2, 1, d) for d in (R, L)),
            ],
        )
        self.task("D3s", ["Dy2"], ["own"], sends=[hop("D", 3, 1, d) for d in (R, L)])
        for (nm, sec), hops in last.items():
            for d in (R, L):
                for h in range(1, hops[d] + 1):
                    more = [hop(nm, sec, h + 1, d)] if h < hops[d] else []
                    self.task(f"{nm}{sec}z{h}{d}", [f"{nm}{sec}z{h}{d}"], ["own"], sends=more)
            for h, (lo, hi) in GROUPS.items():
                got = [f"{nm}{sec}z{h}{d}" for d in (R, L) if h <= hops[d]]
                if not got:
                    continue
                sends = []
                if nm == "X":
                    sends.append(move(f"Xy{h}{R}", ("y", R), "X", 0, 2, lo, hi))
                    sends.append(move(f"Xy{h}{L}", ("y", L), "X", 0, 1, lo, hi))
                sends.append(hand(nm, sec, h, lo, hi))
                if nm == "D" and sec == 2 and h == 3:
                    sends.insert(0, move("Df0", ("y", R), "D", 2, 3, *D_FAR[0]))
                if nm == "D" and sec == 1 and h == 4:
                    got.append("D1g3")
                    sends.insert(0, move("Df1", ("y", L), "D", 1, 3, *D_FAR[1]))
                if nm == "D" and sec > 0:
                    got.append(f"D{sec}s")
                self.task(f"{nm}{sec}g{h}", after=got, sends=sends)
        for h, (lo, hi) in GROUPS.items():
            sends = []
            if h == 1:
                sends.append(move("Xf0", ("y", R), "X", 2, 3, *X_FAR[0]))
            if h == 3:
                sends.append(move("Xf1", ("y", L), "X", 1, 3, *X_FAR[1]))
            if h == 4:
                sends.append(move("Xf2", ("y", R), "X", 2, 3, *X_FAR[2]))
            sends.append(move(f"Xyc{h}", ("p", 0), "X", slice(1, 3), slice(1, 3), lo, hi, (0, 1)))
            prior = ["own"] if h == 1 else [f"Xy{h - 1}"]
            self.task(f"Xy{h}", [f"Xy{h}{R}", f"Xy{h}{L}"], prior, sends=sends)
        for nm, far in (("X", X_FAR), ("D", D_FAR)):
            for i, (lo, hi) in enumerate(far):
                self.task(
                    f"{nm}f{i}", [f"{nm}f{i}"], ["own"], sends=[hand(nm, 3, f"f{i}", lo, hi)]
                )
        self.has = {
            (nm, sec): [
                *(f"{nm}{sec}g{h}" for h in GROUPS if f"{nm}{sec}g{h}" in self.tasks),
                *((f"{nm}f{i}" for i in range(len(far))) if sec == 3 else ()),
                *((f"Xy{h}" for h in GROUPS) if nm == "X" and sec in (1, 2) else ()),
            ]
            for nm, far in (("X", X_FAR), ("D", D_FAR))
            for sec in range(4)
        }
        self.hands = {}
        for (nm, sec), names in self.has.items():
            copies = []
            for n in names:
                copies += [c[0] for c in self.tasks[n][3] if c[1][0] == "p"]
            self.hands[nm, sec] = copies
            at = slice(1, 3) if nm == "X" and sec in (1, 2) else sec
            self.group(f"{nm}{at}", copies, lambda nm=nm, at=at: getattr(k, nm).at[at, :, 1])

    def middle(self):
        k = self.k
        for s, (sec, _, width) in enumerate(CHUNKS):
            w = width / 256
            for j, nm, d, e in ((0, "X", R, L), (1, "D", L, R)):
                self.task(
                    f"m{s}{j}",
                    self.hands[nm, sec],
                    [*self.has[nm, sec], f"t{j}"],
                    lambda s=s, j=j: k.partial(s, j),
                    [
                        (f"r{s}{d}", ("x", d), w / 2,
                         lambda s=s, j=j: (k.at("PB", s).at[j, k.rows("far")], k.at("RL", s).at[j])),
                        (f"f{s}{j}{e}", ("x", e), w / 2,
                         lambda s=s, j=j, e=e: (k.at("PB", s).at[j, k.rows(e)], k.at("FN", s).at[e, j])),
                    ],
                )
                self.task(
                    f"l{s}{j}",
                    [f"r{s}{d}"],
                    [f"m{s}{j}"],
                    lambda s=s, j=j, d=d: k.relay(s, j, d),
                    [
                        (f"f{s}{j}{d}", ("x", d), w / 2,
                         lambda s=s, j=j, d=d: (k.at("PB", s).at[j, k.rows(d)], k.at("FN", s).at[d, j])),
                    ],
                )
            self.group(
                f"f{s}",
                [f"f{s}{j}{d}" for j in range(2) for d in (R, L)],
                lambda s=s: k.at("FN", s),
            )
            for j in range(2):
                if j == 1 and s in DIRECT:
                    continue
                self.group(
                    f"h{s}{j}",
                    [f"h{s}{j}{R}", f"h{s}{j}{L}"],
                    lambda s=s, j=j: k.at("AGB", s).at[j, k.rows("far")],
                )

            def mine(s=s, j=1):
                return (k.at("AGB", s).at[j, k.rows("own")],) * 2

            self.task(
                f"g{s}",
                [f"f{s}{j}{d}" for j in range(2) for d in (R, L)],
                [f"m{s}0", f"m{s}1"],
                lambda s=s: k.gelu(s),
                [(f"a{s}1{d}", ("x", d), w / 2, mine)
                 for d in ((*(("far",) if s in DIRECT else ()), R, L))],
            )
            self.task(
                f"u{s}",
                (),
                [f"g{s}"],
                None,
                [(f"a{s}0{d}", ("x", d), w / 2, lambda s=s: mine(s, 0)) for d in (R, L)],
            )
            for j, before in ((1, f"g{s}"), (0, f"u{s}")):
                for d, e in ((R, L), (L, R)):
                    if j == 1 and s in DIRECT:
                        continue
                    self.task(
                        f"h{s}{j}{d}",
                        [f"a{s}{j}{d}"],
                        [before],
                        None,
                        [
                            (f"h{s}{j}{d}", ("x", d), w / 4,
                             lambda s=s, j=j, d=d, e=e: (k.at("AGB", s).at[j, k.rows(e, d)],) * 2),
                        ],
                    )

    def spread(self, s, j):
        copies = [f"a{s}{j}{d}" for d in (R, L)]
        if j == 1 and s in DIRECT:
            return [*copies, f"a{s}1far"], [f"g{s}"]
        relays = [f"h{s}{j}{d}" for d in (R, L)]
        return copies + relays, relays

    def input_grad(self):
        k = self.k

        def first(s, q, d):
            return 0 if (s + q) % 2 == d else 1

        def start_slot(s, q, d):
            return SUM_SRC[d][first(s, q, d)]

        def half(q):
            return slice(96 * q, 96 * q + 96)

        def zsend(s, q, d, j):
            return (f"S{s}{q}{d}{j}", ("z", d), CHUNKS[s][2] / 512,
                    lambda: (k.at("IGP", s).at[SUM_SRC[d][j], 0, half(q)], k.at("ZR", s).at[d, j, half(q)]))

        def starts(s, q, p):
            return [zsend(s, q, d, first(s, q, d)) for d in (R, L) if start_slot(s, q, d) // 2 == p]

        late = {q for _, q in Y_FIRST}
        for s in range(len(CHUNKS)):
            for p in (3, 2, 1, 0):
                pair = slice(2 * p, 2 * p + 2)
                self.task(
                    f"i{s}{p}",
                    *self.spread(s, 1),
                    lambda s=s, p=p: k.ig_part(s, p),
                    [(f"C{s}{p}", ("p", 0), CHUNKS[s][2] / 128,
                      lambda s=s, pair=pair: (k.at("IGP", s).at[pair, 1], k.at("CR", s).at[pair]))],
                )
                sends = []
                for q in range(2):
                    if (s, q) in Y_FIRST:
                        sends.append((f"A{s}{q}{p}", ("y", s - 1), 1,
                                      lambda s=s, q=q, pair=pair: (k.at("IGP", s).at[pair, 0, half(q)],
                                                                   k.YA.at[s - 1, pair, half(q)])))
                    elif s > 0 or q not in late:
                        sends += starts(s, q, p)
                self.task(
                    f"c{s}{p}", [f"C{s}{p}"], [f"i{s}{p}"], lambda s=s, p=p: k.core_sum(s, p), sends
                )
                for q in sorted(late):
                    if s == 0:
                        froms = [t for t in (1, 2) if (t, q) in Y_FIRST]
                        self.task(
                            f"y{q}{p}",
                            [f"A{t}{q}{p}" for t in froms],
                            [f"c0{p}"] + [f"c{t}{p}" for t in froms],
                            lambda p=p, q=q, froms=froms: k.y_sum(p, half(q), froms),
                            starts(0, q, p),
                        )
        finals = {0: [], 1: []}
        for s in range(len(CHUNKS)):
            for q in range(2):
                if (s, q) in Y_FIRST:
                    continue

                def ready(slot, s=s, q=q):
                    return f"y{q}{slot // 2}" if s == 0 and q in late else f"c{s}{slot // 2}"

                for d in (R, L):
                    for j in range(first(s, q, d), 3):
                        self.task(
                            f"z{s}{q}{d}{j}",
                            [f"S{s}{q}{d}{j}"],
                            [ready(SUM_DST[d][j]), ready(start_slot(s, q, d))],
                            lambda s=s, q=q, d=d, j=j: k.z_sum(s, half(q), d, j),
                            [zsend(s, q, d, j + 1)],
                        )
                sends = []
                if s > 0:
                    link = ("y", (R, L, "far")[CHUNKS[s][0] - 1])
                    finals[q].append(f"F{s}{q}")
                    sends = [(f"F{s}{q}", link, CHUNKS[s][2] / 512,
                              lambda s=s, q=q: (k.at("IGP", s).at[0, 0, half(q)], k.at("YF", s).at[half(q)]))]
                self.task(
                    f"e{s}{q}",
                    [f"S{s}{q}{d}3" for d in (R, L)],
                    [f"z{s}{q}{d}2" for d in (R, L)] + [ready(0)],
                    lambda s=s, q=q: k.z_end(s, half(q)),
                    sends,
                )
        for q in range(2):
            froms = [int(n[1]) for n in finals[q]]
            self.task(
                f"end{q}",
                finals[q],
                [f"e0{q}"] + [f"e{t}{q}" for t in froms],
                lambda q=q, froms=froms: k.end(half(q), froms),
            )

    def weight_grads(self):
        k = self.k
        for s in range(len(CHUNKS)):
            for j in range(2):
                self.task(
                    f"v{s}{j}",
                    *self.spread(s, j),
                    lambda s=s, j=j: k.turn_act(s, j),
                )
        for which, j in ((0, 1), (1, 0)):
            for slot in range(8):
                self.task(
                    f"w{which}{slot}",
                    (),
                    [f"v{s}{j}" for s in range(len(CHUNKS))] + ["t1"],
                    lambda which=which, slot=slot: k.weight_grad(which, slot),
                )


class Device:
    def __init__(self, **refs):
        self.__dict__.update(refs)

    def at(self, name, chunk):
        i = BUFS.index(name)
        return self.wide[i].at[chunk] if chunk < WIDE else self.narrow[i].at[chunk - WIDE]

    def block_rows(self, slot, other):
        row = turn(self.z, Z_REL[slot], self.n_z) * 2 + (1 - self.core if other else self.core)
        return pl.ds(pl.multiple_of(row * 192, 192), 192)

    def load(self):
        self.own = [
            pltpu.make_async_copy(a, b.at[0, 0, 0], self.local_sems.at[i])
            for i, (a, b) in enumerate(((self.x_in, self.X), (self.d_in, self.D)))
        ]
        for copy in self.own:
            copy.start()
        for i, src in enumerate((self.wu_in, self.wd_in)):
            for slot in range(8):
                for other in range(2):
                    rows = pl.ds((slot * 2 + other) * 192, 192)
                    dst = self.WU.at[slot, other] if i == 0 else self.gd_out.at[rows]
                    pltpu.make_async_copy(
                        src.at[self.block_rows(slot, other)], dst, self.local_sems.at[2 + i]
                    ).start()

    def own_wait(self):
        for copy in self.own:
            copy.wait()

    def transpose(self, j):
        src, dst = ((self.WU, self.UT), (self.gd_out, self.DT))[j]
        pltpu.make_async_copy(src, src, self.local_sems.at[2 + j]).wait()

        @pl.loop(0, 4)
        def _(p):
            if j == 0:
                dst[p] = src[pl.ds(p * 2, 2)].reshape(768, 384).T
            else:
                dst[p] = src[pl.ds(pl.multiple_of(p * 768, 768), 768)].T

    def rows(self, which, part=None):
        by = {R: 1, L: -1, "far": 2, "own": 0}[which]
        at = turn(self.c, by, self.n_col) * 96
        if part is None:
            return pl.ds(pl.multiple_of(at, 96), 96)
        return pl.ds(pl.multiple_of(at + 48 * part, 48), 48)

    def partial(self, s, j):
        b, w = ((self.X, self.UT), (self.D, self.DT))[j]
        sec, lane, width = CHUNKS[s]
        acc = jnp.zeros((384, width), f32)
        for p in range(4):
            tokens = b[sec, 2 * p : 2 * p + 2, :, :, lane : lane + width].reshape(768, width)
            acc += jnp.dot(w[p], tokens, preferred_element_type=f32)
        self.at("PB", s)[j] = acc.astype(bf16)

    def relay(self, s, j, d):
        rows = self.rows(d)
        self.at("PB", s)[j, rows] = (
            self.at("PB", s)[j, rows].astype(f32) + self.at("RL", s)[j].astype(f32)
        ).astype(bf16)

    def gelu(self, s):
        rows = self.rows("own")
        pre, back = (
            self.at("PB", s)[j, rows].astype(f32)
            + self.at("FN", s)[0, j].astype(f32)
            + self.at("FN", s)[1, j].astype(f32)
            for j in range(2)
        )
        act, grad = gelu_pair(pre, back)
        self.at("AGB", s)[0, rows] = act.astype(bf16)
        self.at("AGB", s)[1, rows] = grad.astype(bf16)

    def ig_part(self, s, p):
        w = self.WU[2 * p : 2 * p + 2].reshape(768, 384)
        g = jnp.dot(w, self.at("AGB", s)[1], preferred_element_type=f32)
        self.at("IGP", s)[2 * p : 2 * p + 2] = g.astype(bf16).reshape(2, 2, 192, CHUNKS[s][2])

    def core_sum(self, s, p):
        pair = slice(2 * p, 2 * p + 2)
        self.at("IGP", s)[pair, 0] = (
            self.at("IGP", s)[pair, 0].astype(f32) + self.at("CR", s)[pair].astype(f32)
        ).astype(bf16)

    def y_sum(self, p, rows, froms):
        pair = slice(2 * p, 2 * p + 2)
        total = self.at("IGP", 0)[pair, 0, rows].astype(f32)
        for t in froms:
            total += self.YA[t - 1, pair, rows].astype(f32)
        self.at("IGP", 0)[pair, 0, rows] = total.astype(bf16)

    def z_sum(self, s, rows, d, j):
        slot = SUM_DST[d][j]
        self.at("IGP", s)[slot, 0, rows] = (
            self.at("IGP", s)[slot, 0, rows].astype(f32) + self.at("ZR", s)[d, j, rows].astype(f32)
        ).astype(bf16)

    def z_end(self, s, rows):
        total = (
            self.at("IGP", s)[0, 0, rows].astype(f32)
            + self.at("ZR", s)[0, 3, rows].astype(f32)
            + self.at("ZR", s)[1, 3, rows].astype(f32)
        )
        if s == 0:
            self.ig_out[rows] = total
        else:
            self.at("IGP", s)[0, 0, rows] = total.astype(bf16)

    def end(self, rows, froms):
        for t in froms:
            lanes = slice(CHUNKS[t][1], CHUNKS[t][1] + CHUNKS[t][2])
            self.ig_out[rows, lanes] = self.ig_out[rows, lanes] + self.at("YF", t)[rows].astype(f32)

    def turn_act(self, s, j):
        sec, lane, width = CHUNKS[s]
        self.AT[j, sec, lane : lane + width] = self.at("AGB", s)[j].T

    def weight_grad(self, which, slot):
        b, j, out = ((self.X, 1, self.gu_out), (self.D, 0, self.gd_out))[which]
        acc = jnp.zeros((384, 384), f32)
        for s in range(4):
            acc += jnp.dot(
                b[s, slot].reshape(384, 256), self.AT[j, s], preferred_element_type=f32
            )
        acc = acc.astype(bf16)
        out[self.block_rows(slot, 0), :] = acc[:192]
        out[self.block_rows(slot, 1), :] = acc[192:]


def turn(i, by, n):
    return lax.rem(i + (by + n), n)


ORDER = (
    0, 1, 2, 7, 11, 14, 18, 21, 8, 12, 15, 4, 22, 25, 19, 13, 9, 16, 29, 5, 26, 3, 23, 33, 36,
    20, 27, 43, 10, 17, 57, 30, 24, 28, 58, 59, 66, 40, 47, 34, 37, 68, 31, 44, 60, 6, 35, 41,
    48, 38, 69, 67, 82, 32, 39, 45, 74, 61, 76, 51, 53, 55, 70, 42, 49, 71, 46, 50, 83, 62, 75,
    63, 84, 65, 77, 54, 52, 56, 64, 90, 92, 85, 78, 98, 110, 91, 93, 106, 86, 72, 111, 165, 107,
    99, 73, 102, 120, 167, 94, 103, 114, 116, 79, 95, 122, 124, 87, 115, 118, 123, 164, 130,
    132, 126, 125, 131, 134, 133, 117, 128, 88, 100, 81, 136, 169, 80, 135, 171, 89, 96, 156,
    152, 127, 97, 119, 101, 150, 159, 174, 104, 138, 137, 121, 141, 176, 157, 129, 153, 179,
    105, 146, 168, 166, 151, 178, 173, 170, 160, 108, 158, 184, 154, 139, 187, 109, 147, 144,
    180, 172, 177, 161, 142, 112, 140, 155, 182, 148, 113, 145, 181, 175, 185, 183, 186, 143,
    162, 149, 163,
)


def kernel(
    x_in, d_in, wu_in, wd_in,
    ig_out, gu_out, gd_out,
    X, D, WU, UT, DT, AT, YA,
    send_sems, recv_sems, local_sems,
    *chunk_bufs,
):
    refs = dict(locals())
    n_sec, n_row, n_col = (lax.axis_size(a) for a in ("section", "row", "col"))
    n_z = n_row // 2
    s, r, c = (lax.axis_index(a) for a in ("section", "row", "col"))
    z, core = r // 2, r % 2
    device_of = {("p", 0): {"row": z * 2 + (1 - core)}, ("y", "far"): {"section": turn(s, 2, n_sec)}}
    if DIRECT:
        device_of["x", "far"] = {"col": turn(c, 2, n_col)}
    for d, by in ((R, 1), (L, -1)):
        device_of["z", d] = {"row": turn(z, by, n_z) * 2 + core}
        device_of["y", d] = {"section": turn(s, by, n_sec)}
        device_of["x", d] = {"col": turn(c, by, n_col)}

    barrier = pltpu.get_barrier_semaphore()
    for dev in device_of.values():
        pl.semaphore_signal(barrier, inc=1, device_id=dev, device_id_type=pl.DeviceIdType.MESH)
    here = Device(**refs, wide=chunk_bufs[: len(BUFS)], narrow=chunk_bufs[len(BUFS) :], z=z, core=core, c=c, n_z=n_z, n_col=n_col)
    here.load()
    pl.semaphore_wait(barrier, len(device_of))

    plan = Plan(here)
    tasks, groups = plan.tasks, plan.groups
    started, descriptors, done, recv_of, link_of = {}, [], set(), {}, {}
    start_at, arrived, heard = {}, {}, {}
    last_user = []
    names = list(tasks)
    assert sorted(ORDER) == list(range(len(names)))
    for name in (names[i] for i in ORDER):
        needs, after, do, sends = tasks[name]
        assert done.issuperset(after)
        for copy in needs:
            key = groups.get(copy, copy)
            if key not in arrived:
                arrived[key] = len(arrived) + len(descriptors)
                for c in [c for c in started if groups.get(c, c) == key]:
                    heard[link_of[c]] = max(heard.get(link_of[c], -1), start_at[c])
                if key in plan.regions:
                    region = plan.regions[key]()
                    pltpu.make_async_copy(region, region, recv_sems.at[recv_of[key]]).wait()
                else:
                    started[copy].wait_recv()
        if do is not None:
            do()
        for copy, link, _, of in sends:
            src, dst = of()
            i = len(descriptors)
            key = groups.get(copy, copy)
            link_of[copy], start_at[copy] = link, len(arrived) + i
            back = (link[0], 1 - link[1]) if link[0] in "zyx" and link[1] != "far" else link
            if key not in recv_of:
                again = [
                    n
                    for n, user in enumerate(last_user)
                    if key == copy == groups.get(copy, copy)
                    and link_of.get(user) == link
                    and user in arrived
                    and arrived[user] < heard.get(back, -1)
                ]
                if again:
                    recv_of[key] = again[0]
                    last_user[again[0]] = key
                else:
                    recv_of[key] = len(last_user)
                    last_user.append(key)
            if i >= SEND_SEMS:
                descriptors[i - SEND_SEMS].wait_send()
            started[copy] = pltpu.make_async_remote_copy(
                src_ref=src,
                dst_ref=dst,
                send_sem=send_sems.at[i % SEND_SEMS],
                recv_sem=recv_sems.at[recv_of[key]],
                device_id=device_of[link],
                device_id_type=pl.DeviceIdType.MESH,
            )
            started[copy].start()
            descriptors.append(started[copy])
        done.add(name)
    assert set(arrived) == set(recv_of) and len(last_user) <= RECV_SEMS, len(last_user)
    for copy in descriptors[-SEND_SEMS:]:
        copy.wait_send()


def chunk_buffers(n, width):
    shapes = (
        (2, 384),
        (2, 96),
        (2, 2, 96),
        (2, 384),
        (8, 2, 192),
        (8, 192),
        (2, 4, 192),
        (192,),
    )
    return [pltpu.VMEM((n, *shape, width), bf16) for shape in shapes]


def on_device(inputs, out_grad, w_up, w_down):
    any_spec = pl.BlockSpec(memory_space=pl.ANY)
    ig_t, gu, gd = pl.pallas_call(
        kernel,
        out_shape=(
            pltpu.VMEM((192, 256), f32),
            pltpu.VMEM((3072, 384), bf16),
            pltpu.VMEM((3072, 384), bf16),
        ),
        in_specs=[any_spec] * 4,
        out_specs=(pl.BlockSpec(memory_space=pltpu.VMEM),) * 3,
        scratch_shapes=[
            pltpu.VMEM((4, 8, 2, 192, 256), bf16),
            pltpu.VMEM((4, 8, 2, 192, 256), bf16),
            pltpu.VMEM((8, 2, 192, 384), bf16),
            pltpu.VMEM((4, 384, 768), bf16),
            pltpu.VMEM((4, 384, 768), bf16),
            pltpu.VMEM((2, 4, 256, 384), bf16),
            pltpu.VMEM((2, 8, 192, 256), bf16),
            pltpu.SemaphoreType.DMA((SEND_SEMS,)),
            pltpu.SemaphoreType.DMA((RECV_SEMS,)),
            pltpu.SemaphoreType.DMA((4,)),
            *chunk_buffers(WIDE, 256),
            *(chunk_buffers(len(CHUNKS) - WIDE, 128) if len(CHUNKS) > WIDE else ()),
        ],
        compiler_params=pltpu.CompilerParams(
            collective_id=0, has_side_effects=True, vmem_limit_bytes=52 * 2**20
        ),
        cost_estimate=pl.CostEstimate(
            flops=5 * 2 * 1024 * 3072 * 384, bytes_accessed=10_000_000, transcendentals=98304
        ),
        name="ffn_backward",
    )(inputs.T, out_grad.T, w_up, w_down)
    return ig_t.T, gu, gd


def solution(mesh):
    return jax.shard_map(
        on_device,
        mesh=mesh,
        in_specs=(
            P("section", ("col", "row")),
            P("section", ("col", "row")),
            P("col", ("section", "row")),
            P("col", ("section", "row")),
        ),
        out_specs=(
            P("section", ("col", "row")),
            P("col", ("section", "row")),
            P("col", ("section", "row")),
        ),
        check_vma=False,
    )
```

```python
import functools

import jax
import jax.numpy as jnp
from jax import lax
from jax.experimental import pallas as pl
from jax.experimental.pallas import tpu as pltpu
from jax.sharding import PartitionSpec as P

coeff = 0.7978845608028654
f32 = jnp.float32
bf16 = jnp.bfloat16
R, L = 0, 1
SEND_SEMS = 48
RECV_SEMS = 78

Z_REL = (0, 1, -1, 2, -2, 3, -3, 4)
GATHER_SRC = {R: (0, 2, 4, 6), L: (0, 1, 3, 5)}
GATHER_DST = {R: (2, 4, 6, 7), L: (1, 3, 5, 7)}
GROUPS = {1: (0, 3), 2: (3, 5), 3: (5, 7), 4: (7, 8)}
SUM_SRC = {R: (7, 5, 3, 1), L: (7, 6, 4, 2)}
SUM_DST = {R: (5, 3, 1, 0), L: (6, 4, 2, 0)}
X_FAR = ((0, 3), (3, 7), (7, 8))
D_FAR = ((5, 6), (6, 8))
Y_FIRST = ((1, 0), (2, 0), (1, 1), (2, 1))
CHUNKS = ((0, 0, 256), (1, 0, 256), (2, 0, 256), (3, 0, 256))
WIDE = 4
DIRECT = (0, 1, 2, 3)
BUFS = ("PB", "RL", "FN", "AGB", "IGP", "CR", "ZR", "YF")


def gelu_pair(pre, back):
    inner = coeff * (pre + 0.044715 * pre * pre * pre)
    tanh_val = jnp.tanh(inner)
    act = 0.5 * pre * (1.0 + tanh_val)
    slope = 0.5 * (1.0 + tanh_val) + 0.5 * pre * (1.0 - tanh_val * tanh_val) * coeff * (
        1.0 + 3.0 * 0.044715 * pre * pre
    )
    return act, back * slope


class Plan:
    def __init__(self, k):
        self.k = k
        self.tasks = {}
        self.groups = {}
        self.regions = {}
        self.gather()
        self.middle()
        self.input_grad()
        self.weight_grads()

    def group(self, name, copies, region):
        self.groups.update({copy: name for copy in copies})
        self.regions[name] = region

    def task(self, name, needs=(), after=(), do=None, sends=()):
        assert name not in self.tasks
        self.tasks[name] = (tuple(needs), tuple(after), do, tuple(sends))

    def gather(self):
        k = self.k
        last = {("X", 0): (4, 3), ("D", 0): (3, 4), ("D", 1): (4, 3), ("D", 2): (3, 4), ("D", 3): (2, 2)}

        def hop(nm, sec, h, d):
            link = ("z", d)

            def refs():
                b = getattr(k, nm)
                src = b.at[sec, GATHER_SRC[d][h - 1], 0]
                if sec == 0 and h == 1:
                    src = k.x_in if nm == "X" else k.d_in
                return src, b.at[sec, GATHER_DST[d][h - 1], 0]

            return (f"{nm}{sec}z{h}{d}", link, 1, refs)

        def move(name, link, nm, sec, to, lo, hi, half=(0, 0)):
            def refs():
                b = getattr(k, nm)
                return b.at[sec, lo:hi, half[0]], b.at[to, lo:hi, half[1]]

            n = (hi - lo) * (2 if isinstance(sec, slice) else 1)
            return (name, link, n, refs)

        def hand(nm, sec, tag, lo, hi):
            return move(f"{nm}{sec}c{tag}", ("p", 0), nm, sec, sec, lo, hi, (0, 1))

        self.task(
            "go",
            sends=[hop(nm, 0, 1, d) for nm in "XD" for d in (R, L)]
            + [
                ("DyR", ("y", R), 1, lambda: (k.d_in, k.D.at[2, 0, 0])),
                ("DyL", ("y", L), 1, lambda: (k.d_in, k.D.at[1, 0, 0])),
            ],
        )
        self.task("own", after=["go"], do=lambda: k.own_wait())
        for j in range(2):
            self.task(f"t{j}", after=["own"], do=lambda j=j: k.transpose(j))
        self.task("D1s", ["DyL"], ["own"], sends=[hop("D", 1, 1, d) for d in (R, L)])
        self.task(
            "D2s",
            ["DyR"],
            ["own"],
            sends=[
                ("Dy2", ("y", R), 1, lambda: (k.D.at[2, 0, 0], k.D.at[3, 0, 0])),
                *(hop("D", 2, 1, d) for d in (R, L)),
            ],
        )
        self.task("D3s", ["Dy2"], ["own"], sends=[hop("D", 3, 1, d) for d in (R, L)])
        for (nm, sec), hops in last.items():
            for d in (R, L):
                for h in range(1, hops[d] + 1):
                    more = [hop(nm, sec, h + 1, d)] if h < hops[d] else []
                    self.task(f"{nm}{sec}z{h}{d}", [f"{nm}{sec}z{h}{d}"], ["own"], sends=more)
            for h, (lo, hi) in GROUPS.items():
                got = [f"{nm}{sec}z{h}{d}" for d in (R, L) if h <= hops[d]]
                if not got:
                    continue
                sends = []
                if nm == "X":
                    sends.append(move(f"Xy{h}{R}", ("y", R), "X", 0, 2, lo, hi))
                    sends.append(move(f"Xy{h}{L}", ("y", L), "X", 0, 1, lo, hi))
                sends.append(hand(nm, sec, h, lo, hi))
                if nm == "D" and sec == 2 and h == 3:
                    sends.insert(0, move("Df0", ("y", R), "D", 2, 3, *D_FAR[0]))
                if nm == "D" and sec == 1 and h == 4:
                    got.append("D1g3")
                    sends.insert(0, move("Df1", ("y", L), "D", 1, 3, *D_FAR[1]))
                if nm == "D" and sec > 0:
                    got.append(f"D{sec}s")
                self.task(f"{nm}{sec}g{h}", after=got, sends=sends)
        for h, (lo, hi) in GROUPS.items():
            sends = []
            if h == 1:
                sends.append(move("Xf0", ("y", R), "X", 2, 3, *X_FAR[0]))
            if h == 3:
                sends.append(move("Xf1", ("y", L), "X", 1, 3, *X_FAR[1]))
            if h == 4:
                sends.append(move("Xf2", ("y", R), "X", 2, 3, *X_FAR[2]))
            sends.append(move(f"Xyc{h}", ("p", 0), "X", slice(1, 3), slice(1, 3), lo, hi, (0, 1)))
            prior = ["own"] if h == 1 else [f"Xy{h - 1}"]
            self.task(f"Xy{h}", [f"Xy{h}{R}", f"Xy{h}{L}"], prior, sends=sends)
        for nm, far in (("X", X_FAR), ("D", D_FAR)):
            for i, (lo, hi) in enumerate(far):
                self.task(
                    f"{nm}f{i}", [f"{nm}f{i}"], ["own"], sends=[hand(nm, 3, f"f{i}", lo, hi)]
                )
        self.has = {
            (nm, sec): [
                *(f"{nm}{sec}g{h}" for h in GROUPS if f"{nm}{sec}g{h}" in self.tasks),
                *((f"{nm}f{i}" for i in range(len(far))) if sec == 3 else ()),
                *((f"Xy{h}" for h in GROUPS) if nm == "X" and sec in (1, 2) else ()),
            ]
            for nm, far in (("X", X_FAR), ("D", D_FAR))
            for sec in range(4)
        }
        self.hands = {}
        for (nm, sec), names in self.has.items():
            copies = []
            for n in names:
                copies += [c[0] for c in self.tasks[n][3] if c[1][0] == "p"]
            self.hands[nm, sec] = copies
            at = slice(1, 3) if nm == "X" and sec in (1, 2) else sec
            self.group(f"{nm}{at}", copies, lambda nm=nm, at=at: getattr(k, nm).at[at, :, 1])

    def middle(self):
        k = self.k
        for s, (sec, _, width) in enumerate(CHUNKS):
            w = width / 256
            for j, nm, d, e in ((0, "X", R, L), (1, "D", L, R)):
                self.task(
                    f"m{s}{j}",
                    self.hands[nm, sec],
                    [*self.has[nm, sec], f"t{j}"],
                    lambda s=s, j=j: k.partial(s, j),
                    [
                        (f"r{s}{d}", ("x", d), w / 2,
                         lambda s=s, j=j: (k.at("PB", s).at[j, k.rows("far")], k.at("RL", s).at[j])),
                        (f"f{s}{j}{e}", ("x", e), w / 2,
                         lambda s=s, j=j, e=e: (k.at("PB", s).at[j, k.rows(e)], k.at("FN", s).at[e, j])),
                    ],
                )
                self.task(
                    f"l{s}{j}",
                    [f"r{s}{d}"],
                    [f"m{s}{j}"],
                    lambda s=s, j=j, d=d: k.relay(s, j, d),
                    [
                        (f"f{s}{j}{d}", ("x", d), w / 2,
                         lambda s=s, j=j, d=d: (k.at("PB", s).at[j, k.rows(d)], k.at("FN", s).at[d, j])),
                    ],
                )
            self.group(
                f"f{s}",
                [f"f{s}{j}{d}" for j in range(2) for d in (R, L)],
                lambda s=s: k.at("FN", s),
            )
            for j in range(2):
                if j == 1 and s in DIRECT:
                    continue
                self.group(
                    f"h{s}{j}",
                    [f"h{s}{j}{R}", f"h{s}{j}{L}"],
                    lambda s=s, j=j: k.at("AGB", s).at[j, k.rows("far")],
                )

            def mine(s=s, j=1):
                return (k.at("AGB", s).at[j, k.rows("own")],) * 2

            self.task(
                f"g{s}",
                [f"f{s}{j}{d}" for j in range(2) for d in (R, L)],
                [f"m{s}0", f"m{s}1"],
                lambda s=s: k.gelu(s),
                [(f"a{s}1{d}", ("x", d), w / 2, mine)
                 for d in ((*(("far",) if s in DIRECT else ()), R, L))],
            )
            self.task(
                f"u{s}",
                (),
                [f"g{s}"],
                None,
                [(f"a{s}0{d}", ("x", d), w / 2, lambda s=s: mine(s, 0)) for d in (R, L)],
            )
            for j, before in ((1, f"g{s}"), (0, f"u{s}")):
                for d, e in ((R, L), (L, R)):
                    if j == 1 and s in DIRECT:
                        continue
                    self.task(
                        f"h{s}{j}{d}",
                        [f"a{s}{j}{d}"],
                        [before],
                        None,
                        [
                            (f"h{s}{j}{d}", ("x", d), w / 4,
                             lambda s=s, j=j, d=d, e=e: (k.at("AGB", s).at[j, k.rows(e, d)],) * 2),
                        ],
                    )

    def spread(self, s, j):
        copies = [f"a{s}{j}{d}" for d in (R, L)]
        if j == 1 and s in DIRECT:
            return [*copies, f"a{s}1far"], [f"g{s}"]
        relays = [f"h{s}{j}{d}" for d in (R, L)]
        return copies + relays, relays

    def input_grad(self):
        k = self.k

        def first(s, q, d):
            return 0 if (s + q) % 2 == d else 1

        def start_slot(s, q, d):
            return SUM_SRC[d][first(s, q, d)]

        def half(q):
            return slice(96 * q, 96 * q + 96)

        def zsend(s, q, d, j):
            return (f"S{s}{q}{d}{j}", ("z", d), CHUNKS[s][2] / 512,
                    lambda: (k.at("IGP", s).at[SUM_SRC[d][j], 0, half(q)], k.at("ZR", s).at[d, j, half(q)]))

        def starts(s, q, p):
            return [zsend(s, q, d, first(s, q, d)) for d in (R, L) if start_slot(s, q, d) // 2 == p]

        late = {q for _, q in Y_FIRST}
        for s in range(len(CHUNKS)):
            for p in (3, 2, 1, 0):
                pair = slice(2 * p, 2 * p + 2)
                self.task(
                    f"i{s}{p}",
                    *self.spread(s, 1),
                    lambda s=s, p=p: k.ig_part(s, p),
                    [(f"C{s}{p}", ("p", 0), CHUNKS[s][2] / 128,
                      lambda s=s, pair=pair: (k.at("IGP", s).at[pair, 1], k.at("CR", s).at[pair]))],
                )
                sends = []
                for q in range(2):
                    if (s, q) in Y_FIRST:
                        sends.append((f"A{s}{q}{p}", ("y", s - 1), 1,
                                      lambda s=s, q=q, pair=pair: (k.at("IGP", s).at[pair, 0, half(q)],
                                                                   k.YA.at[s - 1, pair, half(q)])))
                    elif s > 0 or q not in late:
                        sends += starts(s, q, p)
                self.task(
                    f"c{s}{p}", [f"C{s}{p}"], [f"i{s}{p}"], lambda s=s, p=p: k.core_sum(s, p), sends
                )
                for q in sorted(late):
                    if s == 0:
                        froms = [t for t in (1, 2) if (t, q) in Y_FIRST]
                        self.task(
                            f"y{q}{p}",
                            [f"A{t}{q}{p}" for t in froms],
                            [f"c0{p}"] + [f"c{t}{p}" for t in froms],
                            lambda p=p, q=q, froms=froms: k.y_sum(p, half(q), froms),
                            starts(0, q, p),
                        )
        finals = {0: [], 1: []}
        for s in range(len(CHUNKS)):
            for q in range(2):
                if (s, q) in Y_FIRST:
                    continue

                def ready(slot, s=s, q=q):
                    return f"y{q}{slot // 2}" if s == 0 and q in late else f"c{s}{slot // 2}"

                for d in (R, L):
                    for j in range(first(s, q, d), 3):
                        self.task(
                            f"z{s}{q}{d}{j}",
                            [f"S{s}{q}{d}{j}"],
                            [ready(SUM_DST[d][j]), ready(start_slot(s, q, d))],
                            lambda s=s, q=q, d=d, j=j: k.z_sum(s, half(q), d, j),
                            [zsend(s, q, d, j + 1)],
                        )
                sends = []
                if s > 0:
                    link = ("y", (R, L, "far")[CHUNKS[s][0] - 1])
                    finals[q].append(f"F{s}{q}")
                    sends = [(f"F{s}{q}", link, CHUNKS[s][2] / 512,
                              lambda s=s, q=q: (k.at("IGP", s).at[0, 0, half(q)], k.at("YF", s).at[half(q)]))]
                self.task(
                    f"e{s}{q}",
                    [f"S{s}{q}{d}3" for d in (R, L)],
                    [f"z{s}{q}{d}2" for d in (R, L)] + [ready(0)],
                    lambda s=s, q=q: k.z_end(s, half(q)),
                    sends,
                )
        for q in range(2):
            froms = [int(n[1]) for n in finals[q]]
            self.task(
                f"end{q}",
                finals[q],
                [f"e0{q}"] + [f"e{t}{q}" for t in froms],
                lambda q=q, froms=froms: k.end(half(q), froms),
            )

    def weight_grads(self):
        k = self.k
        for s in range(len(CHUNKS)):
            for j in range(2):
                self.task(
                    f"v{s}{j}",
                    *self.spread(s, j),
                    lambda s=s, j=j: k.turn_act(s, j),
                )
        for which, j in ((0, 1), (1, 0)):
            for slot in range(8):
                self.task(
                    f"w{which}{slot}",
                    (),
                    [f"v{s}{j}" for s in range(len(CHUNKS))] + ["t1"],
                    lambda which=which, slot=slot: k.weight_grad(which, slot),
                )


class Device:
    def __init__(self, **refs):
        self.__dict__.update(refs)

    def at(self, name, chunk):
        i = BUFS.index(name)
        return self.wide[i].at[chunk] if chunk < WIDE else self.narrow[i].at[chunk - WIDE]

    def block_rows(self, slot, other):
        row = turn(self.z, Z_REL[slot], self.n_z) * 2 + (1 - self.core if other else self.core)
        return pl.ds(pl.multiple_of(row * 192, 192), 192)

    def load(self):
        self.own = [
            pltpu.make_async_copy(a, b.at[0, 0, 0], self.local_sems.at[i])
            for i, (a, b) in enumerate(((self.x_in, self.X), (self.d_in, self.D)))
        ]
        for copy in self.own:
            copy.start()

    def load_weights(self):
        for i, src in enumerate((self.wu_in, self.wd_in)):
            for slot in range(8):
                for other in range(2):
                    rows = pl.ds((slot * 2 + other) * 192, 192)
                    dst = self.WU.at[slot, other] if i == 0 else self.gd_out.at[rows]
                    pltpu.make_async_copy(
                        src.at[self.block_rows(slot, other)], dst, self.local_sems.at[2 + i]
                    ).start()

    def own_wait(self):
        self.load_weights()
        for copy in self.own:
            copy.wait()

    def transpose(self, j):
        src, dst = ((self.WU, self.UT), (self.gd_out, self.DT))[j]
        pltpu.make_async_copy(src, src, self.local_sems.at[2 + j]).wait()

        @pl.loop(0, 4)
        def _(p):
            if j == 0:
                dst[p] = src[pl.ds(p * 2, 2)].reshape(768, 384).T
            else:
                dst[p] = src[pl.ds(pl.multiple_of(p * 768, 768), 768)].T

    def rows(self, which, part=None):
        by = {R: 1, L: -1, "far": 2, "own": 0}[which]
        at = turn(self.c, by, self.n_col) * 96
        if part is None:
            return pl.ds(pl.multiple_of(at, 96), 96)
        return pl.ds(pl.multiple_of(at + 48 * part, 48), 48)

    def partial(self, s, j):
        b, w = ((self.X, self.UT), (self.D, self.DT))[j]
        sec, lane, width = CHUNKS[s]
        acc = jnp.zeros((384, width), f32)
        for p in range(4):
            tokens = b[sec, 2 * p : 2 * p + 2, :, :, lane : lane + width].reshape(768, width)
            acc += jnp.dot(w[p], tokens, preferred_element_type=f32)
        self.at("PB", s)[j] = acc.astype(bf16)

    def relay(self, s, j, d):
        rows = self.rows(d)
        self.at("PB", s)[j, rows] = (
            self.at("PB", s)[j, rows].astype(f32) + self.at("RL", s)[j].astype(f32)
        ).astype(bf16)

    def gelu(self, s):
        rows = self.rows("own")
        pre, back = (
            self.at("PB", s)[j, rows].astype(f32)
            + self.at("FN", s)[0, j].astype(f32)
            + self.at("FN", s)[1, j].astype(f32)
            for j in range(2)
        )
        act, grad = gelu_pair(pre, back)
        self.at("AGB", s)[0, rows] = act.astype(bf16)
        self.at("AGB", s)[1, rows] = grad.astype(bf16)

    def ig_part(self, s, p):
        w = self.WU[2 * p : 2 * p + 2].reshape(768, 384)
        g = jnp.dot(w, self.at("AGB", s)[1], preferred_element_type=f32)
        self.at("IGP", s)[2 * p : 2 * p + 2] = g.astype(bf16).reshape(2, 2, 192, CHUNKS[s][2])

    def core_sum(self, s, p):
        pair = slice(2 * p, 2 * p + 2)
        self.at("IGP", s)[pair, 0] = (
            self.at("IGP", s)[pair, 0].astype(f32) + self.at("CR", s)[pair].astype(f32)
        ).astype(bf16)

    def y_sum(self, p, rows, froms):
        pair = slice(2 * p, 2 * p + 2)
        total = self.at("IGP", 0)[pair, 0, rows].astype(f32)
        for t in froms:
            total += self.YA[t - 1, pair, rows].astype(f32)
        self.at("IGP", 0)[pair, 0, rows] = total.astype(bf16)

    def z_sum(self, s, rows, d, j):
        slot = SUM_DST[d][j]
        self.at("IGP", s)[slot, 0, rows] = (
            self.at("IGP", s)[slot, 0, rows].astype(f32) + self.at("ZR", s)[d, j, rows].astype(f32)
        ).astype(bf16)

    def z_end(self, s, rows):
        total = (
            self.at("IGP", s)[0, 0, rows].astype(f32)
            + self.at("ZR", s)[0, 3, rows].astype(f32)
            + self.at("ZR", s)[1, 3, rows].astype(f32)
        )
        if s == 0:
            self.ig_out[rows] = total
        else:
            self.at("IGP", s)[0, 0, rows] = total.astype(bf16)

    def end(self, rows, froms):
        for t in froms:
            lanes = slice(CHUNKS[t][1], CHUNKS[t][1] + CHUNKS[t][2])
            self.ig_out[rows, lanes] = self.ig_out[rows, lanes] + self.at("YF", t)[rows].astype(f32)

    def turn_act(self, s, j):
        sec, lane, width = CHUNKS[s]
        self.AT[j, sec, lane : lane + width] = self.at("AGB", s)[j].T

    def weight_grad(self, which, slot):
        b, j, out = ((self.X, 1, self.gu_out), (self.D, 0, self.gd_out))[which]
        acc = jnp.zeros((384, 384), f32)
        for s in range(4):
            acc += jnp.dot(
                b[s, slot].reshape(384, 256), self.AT[j, s], preferred_element_type=f32
            )
        acc = acc.astype(bf16)
        out[self.block_rows(slot, 0), :] = acc[:192]
        out[self.block_rows(slot, 1), :] = acc[192:]


def turn(i, by, n):
    return lax.rem(i + (by + n), n)


ORDER = (
    0, 1, 2, 7, 11, 14, 18, 21, 8, 12, 15, 4, 22, 25, 19, 13, 9, 16, 29, 5, 26, 3, 23, 33, 36,
    20, 27, 43, 10, 17, 57, 30, 24, 28, 58, 59, 66, 40, 47, 34, 37, 68, 31, 44, 60, 6, 35, 41,
    48, 38, 69, 67, 82, 32, 39, 45, 74, 61, 76, 51, 53, 55, 70, 42, 49, 71, 46, 50, 83, 62, 75,
    63, 84, 65, 77, 54, 52, 56, 64, 90, 92, 85, 78, 98, 110, 91, 93, 106, 86, 72, 111, 165, 107,
    99, 73, 102, 120, 167, 94, 103, 114, 116, 79, 95, 122, 124, 87, 115, 118, 123, 164, 130,
    132, 126, 125, 131, 134, 133, 117, 128, 88, 100, 81, 136, 169, 80, 135, 171, 89, 96, 156,
    152, 127, 97, 119, 101, 150, 159, 174, 104, 138, 137, 121, 141, 176, 157, 129, 153, 179,
    105, 146, 168, 166, 151, 178, 173, 170, 160, 108, 158, 184, 154, 139, 187, 109, 147, 144,
    180, 172, 177, 161, 142, 112, 140, 155, 182, 148, 113, 145, 181, 175, 185, 183, 186, 143,
    162, 149, 163,
)


def kernel(
    x_in, d_in, wu_in, wd_in,
    ig_out, gu_out, gd_out,
    X, D, WU, UT, DT, AT, YA,
    send_sems, recv_sems, local_sems,
    *chunk_bufs,
):
    refs = dict(locals())
    n_sec, n_row, n_col = (lax.axis_size(a) for a in ("section", "row", "col"))
    n_z = n_row // 2
    s, r, c = (lax.axis_index(a) for a in ("section", "row", "col"))
    z, core = r // 2, r % 2
    device_of = {("p", 0): {"row": z * 2 + (1 - core)}, ("y", "far"): {"section": turn(s, 2, n_sec)}}
    if DIRECT:
        device_of["x", "far"] = {"col": turn(c, 2, n_col)}
    for d, by in ((R, 1), (L, -1)):
        device_of["z", d] = {"row": turn(z, by, n_z) * 2 + core}
        device_of["y", d] = {"section": turn(s, by, n_sec)}
        device_of["x", d] = {"col": turn(c, by, n_col)}

    barrier = pltpu.get_barrier_semaphore()
    for dev in device_of.values():
        pl.semaphore_signal(barrier, inc=1, device_id=dev, device_id_type=pl.DeviceIdType.MESH)
    here = Device(**refs, wide=chunk_bufs[: len(BUFS)], narrow=chunk_bufs[len(BUFS) :], z=z, core=core, c=c, n_z=n_z, n_col=n_col)
    here.load()
    pl.semaphore_wait(barrier, len(device_of))

    plan = Plan(here)
    tasks, groups = plan.tasks, plan.groups
    started, descriptors, done, recv_of, link_of = {}, [], set(), {}, {}
    start_at, arrived, heard = {}, {}, {}
    last_user = []
    names = list(tasks)
    assert sorted(ORDER) == list(range(len(names)))
    for name in (names[i] for i in ORDER):
        needs, after, do, sends = tasks[name]
        assert done.issuperset(after)
        for copy in needs:
            key = groups.get(copy, copy)
            if key not in arrived:
                arrived[key] = len(arrived) + len(descriptors)
                for c in [c for c in started if groups.get(c, c) == key]:
                    heard[link_of[c]] = max(heard.get(link_of[c], -1), start_at[c])
                if key in plan.regions:
                    region = plan.regions[key]()
                    pltpu.make_async_copy(region, region, recv_sems.at[recv_of[key]]).wait()
                else:
                    started[copy].wait_recv()
        if do is not None:
            do()
        for copy, link, _, of in sends:
            src, dst = of()
            i = len(descriptors)
            key = groups.get(copy, copy)
            link_of[copy], start_at[copy] = link, len(arrived) + i
            back = (link[0], 1 - link[1]) if link[0] in "zyx" and link[1] != "far" else link
            if key not in recv_of:
                again = [
                    n
                    for n, user in enumerate(last_user)
                    if key == copy == groups.get(copy, copy)
                    and link_of.get(user) == link
                    and user in arrived
                    and arrived[user] < heard.get(back, -1)
                ]
                if again:
                    recv_of[key] = again[0]
                    last_user[again[0]] = key
                else:
                    recv_of[key] = len(last_user)
                    last_user.append(key)
            if i >= SEND_SEMS:
                descriptors[i - SEND_SEMS].wait_send()
            started[copy] = pltpu.make_async_remote_copy(
                src_ref=src,
                dst_ref=dst,
                send_sem=send_sems.at[i % SEND_SEMS],
                recv_sem=recv_sems.at[recv_of[key]],
                device_id=device_of[link],
                device_id_type=pl.DeviceIdType.MESH,
            )
            started[copy].start()
            descriptors.append(started[copy])
        done.add(name)
    assert set(arrived) == set(recv_of) and len(last_user) <= RECV_SEMS, len(last_user)
    for copy in descriptors[-SEND_SEMS:]:
        copy.wait_send()


def chunk_buffers(n, width):
    shapes = (
        (2, 384),
        (2, 96),
        (2, 2, 96),
        (2, 384),
        (8, 2, 192),
        (8, 192),
        (2, 4, 192),
        (192,),
    )
    return [pltpu.VMEM((n, *shape, width), bf16) for shape in shapes]


def on_device(inputs, out_grad, w_up, w_down):
    any_spec = pl.BlockSpec(memory_space=pl.ANY)
    ig_t, gu, gd = pl.pallas_call(
        kernel,
        out_shape=(
            pltpu.VMEM((192, 256), f32),
            pltpu.VMEM((3072, 384), bf16),
            pltpu.VMEM((3072, 384), bf16),
        ),
        in_specs=[any_spec] * 4,
        out_specs=(pl.BlockSpec(memory_space=pltpu.VMEM),) * 3,
        scratch_shapes=[
            pltpu.VMEM((4, 8, 2, 192, 256), bf16),
            pltpu.VMEM((4, 8, 2, 192, 256), bf16),
            pltpu.VMEM((8, 2, 192, 384), bf16),
            pltpu.VMEM((4, 384, 768), bf16),
            pltpu.VMEM((4, 384, 768), bf16),
            pltpu.VMEM((2, 4, 256, 384), bf16),
            pltpu.VMEM((2, 8, 192, 256), bf16),
            pltpu.SemaphoreType.DMA((SEND_SEMS,)),
            pltpu.SemaphoreType.DMA((RECV_SEMS,)),
            pltpu.SemaphoreType.DMA((4,)),
            *chunk_buffers(WIDE, 256),
            *(chunk_buffers(len(CHUNKS) - WIDE, 128) if len(CHUNKS) > WIDE else ()),
        ],
        compiler_params=pltpu.CompilerParams(
            collective_id=0, has_side_effects=True, vmem_limit_bytes=52 * 2**20
        ),
        cost_estimate=pl.CostEstimate(
            flops=5 * 2 * 1024 * 3072 * 384, bytes_accessed=10_000_000, transcendentals=98304
        ),
        name="ffn_backward",
    )(inputs.T, out_grad.T, w_up, w_down)
    return ig_t.T, gu, gd


def solution(mesh):
    return jax.shard_map(
        on_device,
        mesh=mesh,
        in_specs=(
            P("section", ("col", "row")),
            P("section", ("col", "row")),
            P("col", ("section", "row")),
            P("col", ("section", "row")),
        ),
        out_specs=(
            P("section", ("col", "row")),
            P("col", ("section", "row")),
            P("col", ("section", "row")),
        ),
        check_vma=False,
    )
```
